256 devices in a mesh: vp: 4 (over x), cp: 8 (over z_hi, core), ga: 8 (over y, z_lo).
Axes of the slice: x: 4, y: 4, z: 8 (z_hi: 4, z_lo: 2; z = z_hi * 2 + z_lo), core: 2. Of those that a mesh axis runs over, the one named last changes fastest.
Arguments:
- valence_wavefunction: bfloat16 [512, 24576], P(('vp', 'cp'), 'ga'), may hold values from -6 to 6
- cond_wave: bfloat16 [512, 24576], P(('vp', 'cp'), 'ga'), may hold values from -6 to 6
- screen_basis: bfloat16 [24576, 1024], P('ga'), may hold values from -0.0390625 to 0.0390625
- screen: float32 [1024], replicated, may hold values from 0.01 to 0.1
- coulomb: float32 [1024], replicated, may hold values from 0.02 to 0.2
- window_rows: int32 [2], replicated, may hold values from 0 to 1023
- tile_owner: int32 [192], P(('vp', 'cp')), may hold values from 0 to 4095, as said below
Outputs:
- kernel: float32 [2, 192, 4096], P(None, ('vp', 'cp'), 'ga')
The draws below stay inside these ranges and needn't reach their ends.
Inputs may be any that keep to these rules, and one draw needn't show every extreme that they name: `tile_owner`: distinct pair-block indices; 0 and 4095 both occur.
All inputs are finite; a program needn't handle non-finite values.
Results may differ from the reference program's by a relative error of at most 0.02.
Values may be sent and summed in bfloat16 or wider, within the bound.
No kernel may reach another device: no remote copies, remote signals or barrier semaphores. Data moves between devices by JAX's collectives and lax.ppermute only.
A program may use at most 64 MiB of HBM per device.

```python
import math
import jax
import jax.numpy as jnp
from jax import lax

NV = 512
NC = 512
NG = 24576
R = 1024
TV = 8
TC = 8
G_DEV = 3072
NCT = 64
PAIR_BLOCK_COUNT = 4096
WINDOW_TILE_COUNT = 192
N_GA = 8


def draw_tile_owner(key, part):
    middle_factor = jax.random.permutation(jax.random.fold_in(key, 11), PAIR_BLOCK_COUNT - 2)[:WINDOW_TILE_COUNT - 2].astype(jnp.int32) + 1
    values = jnp.concatenate([jnp.array([0, PAIR_BLOCK_COUNT - 1], jnp.int32), middle_factor])
    band_order = jax.random.permutation(jax.random.fold_in(key, 12), WINDOW_TILE_COUNT)
    return values[band_order]


def shard_levels(own_key, dims, shards, smallest, largest):
    def one(axis_at, blocks):
        heights = jax.random.uniform(jax.random.fold_in(jax.random.fold_in(own_key, 6), axis_at), (blocks,), jnp.float32, smallest / len(shards), largest / len(shards))
        return jnp.repeat(jnp.exp(heights), dims[axis_at] // blocks).reshape((-1,) + (1,) * (len(dims) - axis_at - 1))

    level = one(*shards[0])
    for cut in shards[1:]:
        level = level * one(*cut)
    return level


def noise(own_key, shape, spread, reach, shards=(), dtype=jnp.bfloat16):
    drawn = spread * jax.random.normal(own_key, shape, jnp.float32)
    if shards:
        drawn = drawn * shard_levels(own_key, shape, shards, -0.22, 0.18)
    return jnp.clip(drawn, -reach, reach).astype(dtype)


def setup_inputs(seed: int = 0) -> dict:
    streams_of = jax.random.split(jax.random.key(seed), 8)
    return {
        "valence_wavefunction": noise(streams_of[0], (NV, NG), 1.0, 6.0, ((0, 32), (1, 8))),
        "cond_wave": noise(streams_of[1], (NC, NG), 1.0, 6.0, ((0, 32), (1, 8))),
        "screen_basis": noise(streams_of[2], (NG, R), NG ** -0.5, 0.0390625, ((0, 8),)),
        "screen": jnp.clip(jnp.exp(jax.random.uniform(streams_of[3], (R,), jnp.float32, math.log(0.01), math.log(0.1))), 0.01, 0.1),
        "coulomb": jnp.clip(jnp.exp(jax.random.uniform(streams_of[4], (R,), jnp.float32, math.log(0.02), math.log(0.2))), 0.02, 0.2),
        "window_rows": jax.random.randint(streams_of[5], (2,), 0, PAIR_BLOCK_COUNT // 4).astype(jnp.int32),
        "tile_owner": draw_tile_owner(jax.random.fold_in(streams_of[7], 71), 0),
    }


def band_block(wave, tile_index, span):
    return lax.dynamic_slice_in_dim(wave, (tile_index * span).astype(jnp.int32), span, 0)


def pair_rows(left_wavefunction, right_wave):
    product = left_wavefunction.astype(jnp.float32)[:, None, :] * right_wave.astype(jnp.float32)[None, :, :]
    return product.reshape(-1, left_wavefunction.shape[1]).astype(jnp.bfloat16)


def project(rho, blocks):
    parts = rho.astype(jnp.float32).reshape(rho.shape[0], N_GA, G_DEV)
    partial_value = jnp.einsum("pkg,kgr->kpr", parts, blocks)
    rounded = lax.optimization_barrier(partial_value.astype(jnp.bfloat16))
    return jnp.sum(rounded.astype(jnp.float32), axis=0)


def reference(valence_wavefunction, cond_wave, screen_basis, screen, coulomb, window_rows, tile_owner):
    blocks = screen_basis.astype(jnp.float32).reshape(N_GA, G_DEV, R)
    row_val = [band_block(valence_wavefunction, window_rows[window_row] // NCT, TV) for window_row in range(2)]
    row_cond = [band_block(cond_wave, window_rows[window_row] % NCT, TC) for window_row in range(2)]
    row_proj = [project(pair_rows(row_val[window_row], row_cond[window_row]), blocks) for window_row in range(2)]

    def per_slot(owner_index):
        slot_valence = band_block(valence_wavefunction, owner_index // NCT, TV)
        slot_cond = band_block(cond_wave, owner_index % NCT, TC)
        col_proj = project(pair_rows(slot_valence, slot_cond), blocks)
        results = []
        for window_row in range(2):
            val_proj = project(pair_rows(row_val[window_row], slot_valence), blocks).reshape(TV, TV, R)
            cond_proj = project(pair_rows(row_cond[window_row], slot_cond), blocks).reshape(TC, TC, R)
            exchange_term = jnp.dot(row_proj[window_row] * coulomb[None, :], col_proj.T, precision=lax.Precision.HIGHEST)
            direct_term = jnp.einsum("vwr,cdr->vcwd", val_proj * screen, cond_proj, precision=lax.Precision.HIGHEST)
            total = 2.0 * exchange_term - direct_term.reshape(TV * TC, TV * TC)
            live_tile = owner_index >= window_rows[window_row]
            results.append(jnp.where(live_tile, total, jnp.zeros_like(total)).reshape(-1))
        return jnp.stack(results)

    stacked = lax.map(per_slot, tile_owner)
    return jnp.transpose(stacked, (1, 0, 2))
```

```python
import functools
import jax
import jax.numpy as jnp
from jax import lax
from jax.experimental import pallas as pl
from jax.experimental.pallas import tpu as pltpu
from jax.sharding import PartitionSpec as P

R = 1024
TV = 8
TC = 8
NCT = 64
F32 = jnp.float32
BF16 = jnp.bfloat16


def shift(array, axis, send_to):
    size = lax.axis_size(axis)
    return lax.ppermute(array, axis, [(n, send_to(n)) for n in range(size)])


def bands_of(tile):
    device = tile // 2
    return device // 8, device % 8, tile % 2


def pick_rows(columns, window_rows, j):
    picked = []
    for first, tiles in ((0, window_rows // NCT), (16, window_rows % NCT)):
        for q in range(2):
            at, column, half = bands_of(tiles[q])
            rows = lax.dynamic_slice(
                columns, (at, first + 8 * half, 0), (1, 8, columns.shape[2])
            )[0]
            picked.append(jnp.where(column == j, rows, jnp.zeros_like(rows)))
    return jnp.concatenate(picked, axis=0)


def spread_over_columns(rows, core):
    half = rows.shape[1] // 2
    low, high = rows[:, :half], rows[:, half:]
    mine = jnp.where(core == 0, low, high)
    other = jnp.where(core == 0, high, low)
    mine = mine + shift(other, "cp", lambda n: n ^ 1)
    parts = [shift(mine, "cp", lambda n, s=s: (n + 2 * s) % 8) for s in (1, 2, 3)]
    mine = mine + parts[0] + parts[1] + parts[2]
    other = shift(mine, "cp", lambda n: n ^ 1)
    return jnp.where(
        core == 0,
        jnp.concatenate([mine, other], axis=1),
        jnp.concatenate([other, mine], axis=1),
    )


def pair_block(left, right):
    product = left.astype(F32)[:, None, :] * right.astype(F32)[None, :, :]
    return product.reshape(-1, left.shape[1])


def exchange_kernel(ids_ref, val_ref, cond_ref, w_ref, out_ref):
    slots = ids_ref.shape[0]
    together = 4

    def band_rows(ref, tile):
        at, column, half = bands_of(tile)
        both = ref[column * 4 + at].astype(F32)
        return jnp.where(half == 0, both[:8], both[8:])

    def body(step, carry):
        pairs = []
        for n in range(together):
            owner = ids_ref[step * together + n]
            left = band_rows(val_ref, owner // NCT)
            right = band_rows(cond_ref, owner % NCT)
            pairs.append(pair_block(left, right).astype(BF16))
        pair = jnp.concatenate(pairs, axis=0)
        result = lax.dot_general(
            w_ref[...], pair, (((1,), (1,)), ((), ())), preferred_element_type=F32
        )
        for n in range(together):
            tile = result[:, n * 64 : (n + 1) * 64]
            out_ref[step * together + n] = jnp.concatenate(
                [tile[c * 16 : (c + 1) * 16] for c in range(8)], axis=1
            )
        return carry

    lax.fori_loop(0, slots // together, body, 0)


def exchange_tiles(ids, val_waves, cond_waves, potential):
    slots = ids.shape[0]
    vmem = pl.BlockSpec(memory_space=pltpu.VMEM)
    return pl.pallas_call(
        exchange_kernel,
        out_shape=jax.ShapeDtypeStruct((slots, 16, 512), F32),
        in_specs=[pl.BlockSpec(memory_space=pltpu.SMEM), vmem, vmem, vmem],
        out_specs=vmem,
        compiler_params=pltpu.CompilerParams(vmem_limit_bytes=32 * 2**20),
        cost_estimate=pl.CostEstimate(
            flops=2 * slots * 64 * 128 * 768, bytes_accessed=2**22, transcendentals=0
        ),
    )(ids, val_waves, cond_waves, potential)


def direct_kernel(ids_ref, val_ref, cond_ref, order_ref, exchange_ref, out_ref, held_ref):
    slots = ids_ref.shape[0]
    lane = lax.broadcasted_iota(jnp.int32, (8, 128), 1)

    def lanes_of(ref, tile):
        at, column, half = bands_of(tile)
        first = pl.multiple_of((at * 2 + half) * 128, 128)
        return ref[column, :, pl.ds(first, 128)]

    def body(slot, carry):
        owner = ids_ref[slot]
        left = lanes_of(val_ref, owner // NCT)
        right = lanes_of(cond_ref, owner % NCT)
        tile = lax.dot_general(
            left, right, (((0,), (0,)), ((), ())), preferred_element_type=F32
        )
        rows = []
        for q in range(2):
            blocks = []
            for m in range(4):
                even = tile[q * 64 + m * 16 : q * 64 + m * 16 + 8]
                odd = tile[q * 64 + m * 16 + 8 : q * 64 + m * 16 + 16]
                if q == 0:
                    odd = pltpu.roll(odd, 64, 1)
                else:
                    even = pltpu.roll(even, 64, 1)
                blocks.append(jnp.where(lane < 64, even, odd))
            rows.append(jnp.concatenate(blocks, axis=1))
        held_ref[slot] = jnp.concatenate(rows, axis=0).astype(BF16)
        return carry

    lax.fori_loop(0, slots, body, 0)
    for part in range(4):
        few = slots // 4
        direct = jnp.dot(
            held_ref[part * few : (part + 1) * few].reshape(few * 16, 512),
            order_ref[...],
            preferred_element_type=F32,
        ).reshape(few, 16, 512)
        total = 2.0 * exchange_ref[part * few : (part + 1) * few] - direct
        out_ref[part * few : (part + 1) * few] = total.astype(BF16)


def kernel_tiles(ids, val_proj, cond_proj, order, exchange):
    slots = ids.shape[0]
    vmem = pl.BlockSpec(memory_space=pltpu.VMEM)
    return pl.pallas_call(
        direct_kernel,
        out_shape=jax.ShapeDtypeStruct((slots, 16, 512), BF16),
        in_specs=[pl.BlockSpec(memory_space=pltpu.SMEM), vmem, vmem, vmem, vmem],
        out_specs=vmem,
        scratch_shapes=[pltpu.VMEM((slots, 16, 512), BF16)],
        compiler_params=pltpu.CompilerParams(vmem_limit_bytes=32 * 2**20),
    )(ids, val_proj, cond_proj, order, exchange)


def gather_columns(array):
    step = [array] + [
        shift(array, "cp", lambda n, s=s: (n + 2 * s) % 8) for s in (1, 2, 3)
    ]
    swapped = [shift(a, "cp", lambda n: n ^ 1) for a in step]
    return step, swapped


def shards(valence_wavefunction, cond_wave, screen_basis, screen, coulomb, window_rows, tile_owner):
    i = lax.axis_index("vp")
    j = lax.axis_index("cp")
    k = lax.axis_index("ga")
    core = j % 2
    own_slots = tile_owner.shape[0]
    grid_count = valence_wavefunction.shape[1]
    quarter = grid_count // 4
    rank_quarter = R // 4
    rank_part = rank_quarter // 8

    from_others = jnp.stack(
        [tile_owner] + [shift(tile_owner, "vp", lambda n, s=s: (n + s) % 4) for s in (1, 2, 3)]
    )
    ids = jnp.take(from_others, (i - jnp.arange(4)) % 4, axis=0).reshape(-1)
    waves = jnp.concatenate([valence_wavefunction, cond_wave], axis=0)
    columns = lax.all_gather(waves, "vp", axis=0)

    rows = spread_over_columns(pick_rows(columns, window_rows, j), core)

    quarter_waves = lax.dynamic_slice_in_dim(columns, i * quarter, quarter, 2)
    quarter_waves, rows = lax.optimization_barrier((quarter_waves, rows))
    val_waves = lax.all_gather(quarter_waves[:, :16], "cp", axis=0)
    cond_waves = lax.all_gather(quarter_waves[:, 16:], "cp", axis=0)

    row_val = rows[:16].reshape(2, TV, grid_count).astype(F32)
    row_cond = rows[16:].reshape(2, TC, grid_count).astype(F32)
    col_val = columns[:, :16].reshape(8, TV, grid_count).astype(F32)
    col_cond = columns[:, 16:].reshape(8, TC, grid_count).astype(F32)
    basis_ranks = lax.dynamic_slice_in_dim(screen_basis, i * rank_quarter, rank_quarter, 1)

    def project(pairs, basis):
        flat = pairs.astype(BF16).reshape(-1, grid_count)
        return lax.dot_general(
            basis, flat, (((0,), (1,)), ((), ())), preferred_element_type=F32
        ).astype(BF16)

    val_part = project(col_val[:, None, :, None] * row_val[None, :, None, :], basis_ranks)
    cond_part = project(row_cond[None, :, :, None] * col_cond[:, None, None, :], basis_ranks)
    row_part = project(
        jnp.swapaxes(row_cond, 0, 1)[:, :, None] * row_val[None], screen_basis
    )
    row_part = row_part.reshape(8, 4, rank_part, 128)
    row_part = jnp.swapaxes(row_part, 1, 2).reshape(8, rank_part, 512)
    sent = jnp.concatenate(
        [
            val_part.reshape(8, rank_part, 1024),
            cond_part.reshape(8, rank_part, 1024),
            row_part,
        ],
        axis=2,
    )
    arrived = lax.all_to_all(sent, "ga", split_axis=0, concat_axis=0, tiled=True)
    summed = arrived.astype(F32).sum(axis=0)

    screen_part = lax.dynamic_slice_in_dim(
        screen, i * rank_quarter + k * rank_part, rank_part, 0
    )
    coulomb_part = lax.dynamic_slice_in_dim(coulomb, k * (R // 8), R // 8, 0)
    val_sum = (summed[:, :1024] * screen_part[:, None]).astype(BF16)
    cond_sum = summed[:, 1024:2048].astype(BF16)
    row_sum = summed[:, 2048:].reshape(rank_part, 4, 128)
    row_sum = (row_sum * coulomb_part.reshape(4, rank_part).T[:, :, None]).astype(BF16)

    step, swapped = gather_columns(jnp.stack([val_sum, cond_sum]))

    row_sum = row_sum.reshape(rank_part, 512)
    row_all = lax.all_to_all(
        jnp.broadcast_to(row_sum[None], (8, rank_part, 512)),
        "ga", split_axis=0, concat_axis=0, tiled=True,
    )
    row_all = jnp.swapaxes(row_all.reshape(8, rank_part, 4, 128), 1, 2).reshape(R, 128)
    basis_rows = lax.dynamic_slice_in_dim(screen_basis, i * quarter, quarter, 0)
    potential = lax.dot_general(
        row_all, basis_rows, (((0,), (1,)), ((), ())), preferred_element_type=F32
    ).astype(BF16)
    exchange = exchange_tiles(
        ids,
        val_waves.reshape(32, 16, quarter),
        cond_waves.reshape(32, 16, quarter),
        potential,
    )

    listed = jnp.stack([a for two in zip(step, swapped) for a in two])
    at = jnp.arange(8, dtype=jnp.int32)
    where_from = ((j // 2 - at // 2) % 4) * 2 + ((j + at) % 2)
    place = jnp.argmax((where_from[None, :] == at[:, None]).astype(jnp.int32), axis=1)
    all_proj = jnp.take(listed, place, axis=0)
    order = jnp.arange(512, dtype=jnp.int32)
    source = (order // 8 % 8) * 64 + (order // 64) * 8 + order % 8
    order = (order[:, None] == source[None, :]).astype(BF16)
    tiles = kernel_tiles(ids, all_proj[:, 0], all_proj[:, 1], order, exchange)

    tiles = tiles.reshape(4, own_slots, 2, 8, 512)
    tiles = jnp.transpose(tiles, (0, 3, 2, 1, 4)).reshape(32, 2 * own_slots, 512)
    got = lax.all_to_all(tiles, ("vp", "ga"), split_axis=0, concat_axis=0, tiled=True)
    kernel = got.astype(F32).sum(axis=0).reshape(2, own_slots, 512)
    live_tile = (tile_owner[None, :] >= window_rows[:, None])[:, :, None]
    return jnp.where(live_tile, kernel, jnp.zeros_like(kernel))


def solution(mesh):
    in_specs = (
        P(("vp", "cp"), "ga"),
        P(("vp", "cp"), "ga"),
        P("ga", None),
        P(),
        P(),
        P(),
        P(("vp", "cp")),
    )
    out_specs = P(None, ("vp", "cp"), "ga")
    return jax.shard_map(shards, mesh=mesh, in_specs=in_specs, out_specs=out_specs, check_vma=False)
```

```python
import functools
import jax
import jax.numpy as jnp
from jax import lax
from jax.experimental import pallas as pl
from jax.experimental.pallas import tpu as pltpu
from jax.sharding import PartitionSpec as P

R = 1024
TV = 8
TC = 8
NCT = 64
F32 = jnp.float32
BF16 = jnp.bfloat16


def shift(array, axis, send_to):
    size = lax.axis_size(axis)
    return lax.ppermute(array, axis, [(n, send_to(n)) for n in range(size)])


def bands_of(tile):
    device = tile // 2
    return device // 8, device % 8, tile % 2


def pick_kernel(meta_ref, window_ref, columns_ref, mine_ref, other_ref):
    i, j = meta_ref[0], meta_ref[1]
    width = 2 * mine_ref.shape[1]
    first_lane = pl.multiple_of(i * width, 128)
    picked = []
    for first in (0, 16):
        for q in range(2):
            block = window_ref[q]
            at, column, half = bands_of(block // NCT if first == 0 else block % NCT)
            both = columns_ref[at, first : first + 16, pl.ds(first_lane, width)].astype(F32)
            rows = jnp.where(half == 0, both[:8], both[8:])
            picked.append(jnp.where(column == j, rows, jnp.zeros_like(rows)))
    rows = jnp.concatenate(picked, axis=0)
    low, high = rows[:, : width // 2], rows[:, width // 2 :]
    mine_ref[...] = jnp.where(j % 2 == 0, low, high).astype(BF16)
    other_ref[...] = jnp.where(j % 2 == 0, high, low).astype(BF16)


def place_kernel(meta_ref, *refs):
    i, j = meta_ref[0], meta_ref[1]
    out_ref = refs[-1]
    width = refs[0].shape[1]
    for n in range(4):
        start = ((i + 4 - n) % 4) * 2
        for flip in range(2):
            first = pl.multiple_of((start + (j + flip) % 2) * width, 128)
            out_ref[:, pl.ds(first, width)] = refs[4 * flip + n][...]


def row_tiles(meta, window_rows, columns):
    width = columns.shape[2] // 8
    smem, vmem = (pl.BlockSpec(memory_space=m) for m in (pltpu.SMEM, pltpu.VMEM))
    part = jax.ShapeDtypeStruct((32, width), BF16)
    mine, other = pl.pallas_call(
        pick_kernel,
        out_shape=(part, part),
        in_specs=[smem, smem, vmem],
        out_specs=(vmem, vmem),
        compiler_params=pltpu.CompilerParams(vmem_limit_bytes=16 * 2**20),
    )(meta, window_rows, columns)
    mine = mine + shift(other, "cp", lambda n: n ^ 1)
    parts = [shift(mine, "cp", lambda n, s=s: (n + 2 * s) % 8) for s in (1, 2, 3)]
    mine = mine + parts[0] + parts[1] + parts[2]
    mine = [mine] + [shift(mine, "vp", lambda n, s=s: (n + s) % 4) for s in (1, 2, 3)]
    other = [shift(a, "cp", lambda n: n ^ 1) for a in mine]
    return pl.pallas_call(
        place_kernel,
        out_shape=jax.ShapeDtypeStruct((32, columns.shape[2]), BF16),
        in_specs=[smem] + [vmem] * 8,
        out_specs=vmem,
        compiler_params=pltpu.CompilerParams(vmem_limit_bytes=16 * 2**20),
    )(meta, *mine, *other)


def pair_block(left, right):
    product = left.astype(F32)[:, None, :] * right.astype(F32)[None, :, :]
    return product.reshape(-1, left.shape[1])


def owner_of(ids_ref, i, slot):
    own = ids_ref.shape[1]
    return ids_ref[(i + 4 - slot // own) % 4, slot % own]


def exchange_kernel(meta_ref, ids_ref, waves_ref, basis_ref, *refs):
    pieces, out_ref = refs[:8], refs[8]
    i, k = meta_ref[0], meta_ref[2]
    together = 4
    potential = None
    for flip in range(2):
        for n in range(4):
            source = ((k // 2 + 4 - n) % 4) * 2 + (k + flip) % 2
            piece = pieces[4 * flip + n][...]
            ranks = jnp.concatenate(
                [piece[:, m * 128 : (m + 1) * 128] for m in range(4)], axis=0
            )
            basis = basis_ref[:, pl.ds(pl.multiple_of(source * 128, 128), 128)]
            term = lax.dot_general(
                ranks, basis, (((0,), (1,)), ((), ())), preferred_element_type=F32
            )
            potential = term if potential is None else potential + term
    potential = potential.astype(BF16)

    def band_rows(first, tile):
        at, column, half = bands_of(tile)
        both = waves_ref[column * 4 + at, first : first + 16].astype(F32)
        return jnp.where(half == 0, both[:8], both[8:])

    for step in range(out_ref.shape[0] // together):
        pairs = []
        for n in range(together):
            owner = owner_of(ids_ref, i, step * together + n)
            left = band_rows(0, owner // NCT)
            right = band_rows(16, owner % NCT)
            pairs.append(pair_block(left, right).astype(BF16))
        pair = jnp.concatenate(pairs, axis=0)
        result = lax.dot_general(
            potential, pair, (((1,), (1,)), ((), ())), preferred_element_type=F32
        )
        for n in range(together):
            tile = result[:, n * 64 : (n + 1) * 64]
            out_ref[step * together + n] = jnp.concatenate(
                [tile[c * 16 : (c + 1) * 16] for c in range(8)], axis=1
            )


def exchange_tiles(meta, ids, waves, basis_rows, pieces):
    slots = 4 * ids.shape[1]
    smem, vmem = (pl.BlockSpec(memory_space=m) for m in (pltpu.SMEM, pltpu.VMEM))
    return pl.pallas_call(
        exchange_kernel,
        out_shape=jax.ShapeDtypeStruct((slots, 16, 512), F32),
        in_specs=[smem, smem, vmem, vmem] + [vmem] * 8,
        out_specs=vmem,
        compiler_params=pltpu.CompilerParams(vmem_limit_bytes=32 * 2**20),
        cost_estimate=pl.CostEstimate(
            flops=2 * slots * 64 * 128 * 768, bytes_accessed=2**22, transcendentals=0
        ),
    )(meta, ids, waves, basis_rows, *pieces)


def direct_kernel(meta_ref, ids_ref, order_ref, exchange_ref, *refs):
    pieces, (out_ref, proj_ref, held_ref, total_ref) = refs[:8], refs[8:]
    i, j = meta_ref[0], meta_ref[1]
    own = ids_ref.shape[1]
    slots = 4 * own
    lane = lax.broadcasted_iota(jnp.int32, (8, 128), 1)
    for flip in range(2):
        for n in range(4):
            source = ((j // 2 + 4 - n) % 4) * 2 + (j + flip) % 2
            proj_ref[source] = pieces[4 * flip + n][...]

    def lanes_of(part, tile):
        at, column, half = bands_of(tile)
        first = pl.multiple_of((at * 2 + half) * 128, 128)
        return proj_ref[column, part, :, pl.ds(first, 128)]

    for slot in range(slots):
        owner = owner_of(ids_ref, i, slot)
        left = lanes_of(0, owner // NCT)
        right = lanes_of(1, owner % NCT)
        tile = lax.dot_general(
            left, right, (((0,), (0,)), ((), ())), preferred_element_type=F32
        )
        rows = []
        for q in range(2):
            blocks = []
            for m in range(4):
                even = tile[q * 64 + m * 16 : q * 64 + m * 16 + 8]
                odd = tile[q * 64 + m * 16 + 8 : q * 64 + m * 16 + 16]
                if q == 0:
                    odd = pltpu.roll(odd, 64, 1)
                else:
                    even = pltpu.roll(even, 64, 1)
                blocks.append(jnp.where(lane < 64, even, odd))
            rows.append(jnp.concatenate(blocks, axis=1))
        held_ref[slot] = jnp.concatenate(rows, axis=0).astype(BF16)
    for part in range(4):
        direct = jnp.dot(
            held_ref[part * own : (part + 1) * own].reshape(own * 16, 512),
            order_ref[...],
            preferred_element_type=F32,
        ).reshape(own, 16, 512)
        total = 2.0 * exchange_ref[part * own : (part + 1) * own] - direct
        for n in range(own):
            for q in range(2):
                total_ref[part * 8 : (part + 1) * 8, q * own + n, :] = total[
                    n, q * 8 : (q + 1) * 8
                ]
    out_ref[...] = total_ref[...].astype(BF16)


def kernel_tiles(meta, ids, order, exchange, pieces):
    own = ids.shape[1]
    slots = 4 * own
    smem, vmem = (pl.BlockSpec(memory_space=m) for m in (pltpu.SMEM, pltpu.VMEM))
    return pl.pallas_call(
        direct_kernel,
        out_shape=jax.ShapeDtypeStruct((32, 2 * own, 512), BF16),
        in_specs=[smem, smem, vmem, vmem] + [vmem] * 8,
        out_specs=vmem,
        scratch_shapes=[
            pltpu.VMEM((8,) + pieces[0].shape, BF16),
            pltpu.VMEM((slots, 16, 512), BF16),
            pltpu.VMEM((32, 2 * own, 512), F32),
        ],
        compiler_params=pltpu.CompilerParams(vmem_limit_bytes=32 * 2**20),
    )(meta, ids, order, exchange, *pieces)


def gather_pieces(array, axis):
    step = [array] + [
        shift(array, axis, lambda n, s=s: (n + 2 * s) % 8) for s in (1, 2, 3)
    ]
    return step + [shift(a, axis, lambda n: n ^ 1) for a in step]


def shards(valence_wavefunction, cond_wave, screen_basis, screen, coulomb, window_rows, tile_owner):
    i = lax.axis_index("vp")
    j = lax.axis_index("cp")
    k = lax.axis_index("ga")
    meta = jnp.stack([i, j, k]).astype(jnp.int32)
    own_slots = tile_owner.shape[0]
    grid_count = valence_wavefunction.shape[1]
    quarter = grid_count // 4
    rank_quarter = R // 4
    rank_part = rank_quarter // 8

    ids = jnp.stack(
        [tile_owner] + [shift(tile_owner, "vp", lambda n, s=s: (n + s) % 4) for s in (1, 2, 3)]
    )
    waves = jnp.concatenate([valence_wavefunction, cond_wave], axis=0)
    columns = lax.all_gather(waves, "vp", axis=0)
    rows = row_tiles(meta, window_rows, columns)

    quarter_waves = lax.dynamic_slice_in_dim(columns, i * quarter, quarter, 2)
    all_waves = lax.all_gather(quarter_waves, "cp", axis=0)

    row_val = rows[:16].reshape(2, TV, grid_count).astype(F32)
    row_cond = rows[16:].reshape(2, TC, grid_count).astype(F32)
    col_val = columns[:, :16].reshape(8, TV, grid_count).astype(F32)
    col_cond = columns[:, 16:].reshape(8, TC, grid_count).astype(F32)
    basis_ranks = lax.dynamic_slice_in_dim(screen_basis, i * rank_quarter, rank_quarter, 1)

    def project(pairs, basis):
        flat = pairs.astype(BF16).reshape(-1, grid_count)
        return lax.dot_general(
            basis, flat, (((0,), (1,)), ((), ())), preferred_element_type=F32
        ).astype(BF16)

    val_part = project(col_val[:, None, :, None] * row_val[None, :, None, :], basis_ranks)
    cond_part = project(row_cond[None, :, :, None] * col_cond[:, None, None, :], basis_ranks)
    row_part = project(
        jnp.swapaxes(row_cond, 0, 1)[:, :, None] * row_val[None], screen_basis
    )
    row_part = row_part.reshape(8, 4, rank_part, 128)
    row_part = jnp.swapaxes(row_part, 1, 2).reshape(8, rank_part, 512)
    sent = jnp.concatenate(
        [
            val_part.reshape(8, rank_part, 1024),
            cond_part.reshape(8, rank_part, 1024),
            row_part,
        ],
        axis=2,
    )
    arrived = lax.all_to_all(sent, "ga", split_axis=0, concat_axis=0, tiled=True)
    summed = arrived.astype(F32).sum(axis=0)

    screen_part = lax.dynamic_slice_in_dim(
        screen, i * rank_quarter + k * rank_part, rank_part, 0
    )
    coulomb_part = lax.dynamic_slice_in_dim(coulomb, k * (R // 8), R // 8, 0)
    val_sum = (summed[:, :1024] * screen_part[:, None]).astype(BF16)
    cond_sum = summed[:, 1024:2048].astype(BF16)
    row_sum = summed[:, 2048:].reshape(rank_part, 4, 128)
    row_sum = (row_sum * coulomb_part.reshape(4, rank_part).T[:, :, None]).astype(BF16)

    proj_pieces = gather_pieces(jnp.stack([val_sum, cond_sum]), "cp")
    row_pieces = gather_pieces(row_sum.reshape(rank_part, 512), "ga")
    basis_rows = lax.dynamic_slice_in_dim(screen_basis, i * quarter, quarter, 0)
    exchange = exchange_tiles(
        meta, ids, all_waves.reshape(32, 32, quarter), basis_rows, row_pieces
    )

    order = jnp.arange(512, dtype=jnp.int32)
    source = (order // 8 % 8) * 64 + (order // 64) * 8 + order % 8
    order = (order[:, None] == source[None, :]).astype(BF16)
    tiles = kernel_tiles(meta, ids, order, exchange, proj_pieces)
    got = lax.all_to_all(tiles, ("vp", "ga"), split_axis=0, concat_axis=0, tiled=True)
    kernel = got.astype(F32).sum(axis=0).reshape(2, own_slots, 512)
    live_tile = (tile_owner[None, :] >= window_rows[:, None])[:, :, None]
    return jnp.where(live_tile, kernel, jnp.zeros_like(kernel))


def solution(mesh):
    in_specs = (
        P(("vp", "cp"), "ga"),
        P(("vp", "cp"), "ga"),
        P("ga", None),
        P(),
        P(),
        P(),
        P(("vp", "cp")),
    )
    out_specs = P(None, ("vp", "cp"), "ga")
    return jax.shard_map(shards, mesh=mesh, in_specs=in_specs, out_specs=out_specs, check_vma=False)
```

```python
import functools
import jax
import jax.numpy as jnp
from jax import lax
from jax.experimental import pallas as pl
from jax.experimental.pallas import tpu as pltpu
from jax.sharding import PartitionSpec as P

R = 1024
TV = 8
TC = 8
NCT = 64
F32 = jnp.float32
BF16 = jnp.bfloat16


def shift(array, axis, send_to):
    size = lax.axis_size(axis)
    return lax.ppermute(array, axis, [(n, send_to(n)) for n in range(size)])


def bands_of(tile):
    device = tile // 2
    return device // 8, device % 8, tile % 2


def pick_kernel(meta_ref, window_ref, columns_ref, mine_ref, other_ref, quarter_ref):
    i, j = meta_ref[0], meta_ref[1]
    width = 2 * mine_ref.shape[1]
    first_lane = pl.multiple_of(i * width, 128)
    picked = []
    for first in (0, 16):
        for q in range(2):
            block = window_ref[q]
            at, column, half = bands_of(block // NCT if first == 0 else block % NCT)
            both = columns_ref[at, first : first + 16, pl.ds(first_lane, width)].astype(F32)
            rows = jnp.where(half == 0, both[:8], both[8:])
            picked.append(jnp.where(column == j, rows, jnp.zeros_like(rows)))
    quarter_ref[...] = columns_ref[:, :, pl.ds(first_lane, width)]
    rows = jnp.concatenate(picked, axis=0)
    low, high = rows[:, : width // 2], rows[:, width // 2 :]
    mine_ref[...] = jnp.where(j % 2 == 0, low, high).astype(BF16)
    other_ref[...] = jnp.where(j % 2 == 0, high, low).astype(BF16)


def place_kernel(meta_ref, near_ref, next_ref, far_ref, out_ref):
    i, j = meta_ref[0], meta_ref[1]
    width = out_ref.shape[1] // 8
    for n, flip in enumerate((0, 1, 3, 2)):
        for half in range(2):
            start = (i ^ flip) * 2 + (j + half) % 2
            ref, at = ((near_ref, 0), (next_ref, 0), (far_ref, 0), (far_ref, 2))[n]
            at = (at + half) * width
            first = pl.multiple_of(start * width, 128)
            out_ref[:, pl.ds(first, width)] = ref[:, at : at + width]


def row_tiles(meta, window_rows, columns):
    width = columns.shape[2] // 8
    smem, vmem = (pl.BlockSpec(memory_space=m) for m in (pltpu.SMEM, pltpu.VMEM))
    part = jax.ShapeDtypeStruct((32, width), BF16)
    mine, other, quarter = pl.pallas_call(
        pick_kernel,
        out_shape=(part, part, jax.ShapeDtypeStruct((4, 32, 2 * width), BF16)),
        in_specs=[smem, smem, vmem],
        out_specs=(vmem, vmem, vmem),
        compiler_params=pltpu.CompilerParams(vmem_limit_bytes=16 * 2**20),
    )(meta, window_rows, columns)
    mine = mine + shift(other, "cp", lambda n: n ^ 1)
    mine = mine + shift(mine, "cp", lambda n: n ^ 2)
    mine = mine + shift(mine, "cp", lambda n: n ^ 6)
    quarter, mine = lax.optimization_barrier((quarter, mine))
    near = jnp.concatenate([mine, shift(mine, "cp", lambda n: n ^ 1)], axis=1)
    beside = shift(near, "vp", lambda n: n ^ 1)
    far = shift(jnp.concatenate([near, beside], axis=1), "vp", lambda n: n ^ 3)
    rows = pl.pallas_call(
        place_kernel,
        out_shape=jax.ShapeDtypeStruct((32, columns.shape[2]), BF16),
        in_specs=[smem] + [vmem] * 3,
        out_specs=vmem,
        compiler_params=pltpu.CompilerParams(vmem_limit_bytes=16 * 2**20),
    )(meta, near, beside, far)
    return rows, quarter


def pair_block(left, right):
    product = left.astype(F32)[:, None, :] * right.astype(F32)[None, :, :]
    return product.reshape(-1, left.shape[1])


def owner_of(ids_ref, i, slot):
    own = ids_ref.shape[1]
    return ids_ref[(i + 4 - slot // own) % 4, slot % own]


def exchange_kernel(meta_ref, ids_ref, basis_ref, near_ref, far_ref, *refs):
    pieces, (out_ref, waves_ref) = refs[:8], refs[8:]
    i, j, k = meta_ref[0], meta_ref[1], meta_ref[2]
    together = 4
    potential = None
    for n in range(8):
        source = k ^ (n % 2) ^ (n // 2 % 2 * 2) ^ (n // 4 * 6)
        piece = near_ref[n] if n < 4 else far_ref[n - 4]
        ranks = jnp.concatenate([piece[:, m * 128 : (m + 1) * 128] for m in range(4)], axis=0)
        basis = basis_ref[:, pl.ds(pl.multiple_of(source * 128, 128), 128)]
        term = lax.dot_general(
            ranks, basis, (((0,), (1,)), ((), ())), preferred_element_type=F32
        )
        potential = term if potential is None else potential + term
    for flip in range(2):
        for n in range(4):
            source = ((j // 2 + 4 - n) % 4) * 2 + (j + flip) % 2
            waves_ref[pl.ds(source * 4, 4)] = pieces[4 * flip + n][...]
    potential = potential.astype(BF16)

    def band_rows(first, tile):
        at, column, half = bands_of(tile)
        both = waves_ref[column * 4 + at, first : first + 16].astype(F32)
        return jnp.where(half == 0, both[:8], both[8:])

    for step in range(out_ref.shape[0] // together):
        pairs = []
        for n in range(together):
            owner = owner_of(ids_ref, i, step * together + n)
            left = band_rows(0, owner // NCT)
            right = band_rows(16, owner % NCT)
            pairs.append(pair_block(left, right).astype(BF16))
        pair = jnp.concatenate(pairs, axis=0)
        result = lax.dot_general(
            potential, pair, (((1,), (1,)), ((), ())), preferred_element_type=F32
        )
        for n in range(together):
            tile = result[:, n * 64 : (n + 1) * 64]
            out_ref[step * together + n] = jnp.concatenate(
                [tile[c * 16 : (c + 1) * 16] for c in range(8)], axis=1
            )


def exchange_tiles(meta, ids, basis_rows, near, far, pieces):
    slots = 4 * ids.shape[1]
    smem, vmem = (pl.BlockSpec(memory_space=m) for m in (pltpu.SMEM, pltpu.VMEM))
    return pl.pallas_call(
        exchange_kernel,
        out_shape=jax.ShapeDtypeStruct((slots, 16, 512), F32),
        in_specs=[smem, smem, vmem, vmem, vmem] + [vmem] * 8,
        out_specs=vmem,
        scratch_shapes=[pltpu.VMEM((32,) + pieces[0].shape[1:], BF16)],
        compiler_params=pltpu.CompilerParams(vmem_limit_bytes=32 * 2**20),
        cost_estimate=pl.CostEstimate(
            flops=2 * slots * 64 * 128 * 768, bytes_accessed=2**22, transcendentals=0
        ),
    )(meta, ids, basis_rows, near, far, *pieces)


def direct_kernel(meta_ref, ids_ref, order_ref, exchange_ref, *refs):
    pieces, (out_ref, proj_ref, held_ref, total_ref) = refs[:8], refs[8:]
    i, j = meta_ref[0], meta_ref[1]
    own = ids_ref.shape[1]
    slots = 4 * own
    lane = lax.broadcasted_iota(jnp.int32, (8, 128), 1)
    for flip in range(2):
        for n in range(4):
            source = ((j // 2 + 4 - n) % 4) * 2 + (j + flip) % 2
            proj_ref[source] = pieces[4 * flip + n][...]

    def lanes_of(part, tile):
        at, column, half = bands_of(tile)
        first = pl.multiple_of((at * 2 + half) * 128, 128)
        return proj_ref[column, part, :, pl.ds(first, 128)]

    for slot in range(slots):
        owner = owner_of(ids_ref, i, slot)
        left = lanes_of(0, owner // NCT)
        right = lanes_of(1, owner % NCT)
        tile = lax.dot_general(
            left, right, (((0,), (0,)), ((), ())), preferred_element_type=F32
        )
        rows = []
        for q in range(2):
            blocks = []
            for m in range(4):
                even = tile[q * 64 + m * 16 : q * 64 + m * 16 + 8]
                odd = tile[q * 64 + m * 16 + 8 : q * 64 + m * 16 + 16]
                if q == 0:
                    odd = pltpu.roll(odd, 64, 1)
                else:
                    even = pltpu.roll(even, 64, 1)
                blocks.append(jnp.where(lane < 64, even, odd))
            rows.append(jnp.concatenate(blocks, axis=1))
        held_ref[slot] = jnp.concatenate(rows, axis=0).astype(BF16)
    for part in range(4):
        direct = jnp.dot(
            held_ref[part * own : (part + 1) * own].reshape(own * 16, 512),
            order_ref[...],
            preferred_element_type=F32,
        ).reshape(own, 16, 512)
        total = 2.0 * exchange_ref[part * own : (part + 1) * own] - direct
        for n in range(own):
            for q in range(2):
                total_ref[part * 8 : (part + 1) * 8, q * own + n, :] = total[
                    n, q * 8 : (q + 1) * 8
                ]
    out_ref[...] = total_ref[...].astype(BF16)


def kernel_tiles(meta, ids, order, exchange, pieces):
    own = ids.shape[1]
    slots = 4 * own
    smem, vmem = (pl.BlockSpec(memory_space=m) for m in (pltpu.SMEM, pltpu.VMEM))
    return pl.pallas_call(
        direct_kernel,
        out_shape=jax.ShapeDtypeStruct((32, 2 * own, 512), BF16),
        in_specs=[smem, smem, vmem, vmem] + [vmem] * 8,
        out_specs=vmem,
        scratch_shapes=[
            pltpu.VMEM((8,) + pieces[0].shape, BF16),
            pltpu.VMEM((slots, 16, 512), BF16),
            pltpu.VMEM((32, 2 * own, 512), F32),
        ],
        compiler_params=pltpu.CompilerParams(vmem_limit_bytes=32 * 2**20),
    )(meta, ids, order, exchange, *pieces)


def gather_pieces(array, axis):
    step = [array] + [
        shift(array, axis, lambda n, s=s: (n + 2 * s) % 8) for s in (1, 2, 3)
    ]
    return step + [shift(a, axis, lambda n: n ^ 1) for a in step]


def shards(valence_wavefunction, cond_wave, screen_basis, screen, coulomb, window_rows, tile_owner):
    i = lax.axis_index("vp")
    j = lax.axis_index("cp")
    k = lax.axis_index("ga")
    meta = jnp.stack([i, j, k]).astype(jnp.int32)
    own_slots = tile_owner.shape[0]
    grid_count = valence_wavefunction.shape[1]
    quarter = grid_count // 4
    rank_quarter = R // 4
    rank_part = rank_quarter // 8

    ids = jnp.stack(
        [tile_owner] + [shift(tile_owner, "vp", lambda n, s=s: (n + s) % 4) for s in (1, 2, 3)]
    )
    waves = jnp.concatenate([valence_wavefunction, cond_wave], axis=0)
    columns = lax.all_gather(waves, "vp", axis=0)
    rows, quarter_waves = row_tiles(meta, window_rows, columns)
    wave_pieces = gather_pieces(quarter_waves, "cp")

    row_val = rows[:16].reshape(2, TV, grid_count).astype(F32)
    row_cond = rows[16:].reshape(2, TC, grid_count).astype(F32)
    col_val = columns[:, :16].reshape(8, TV, grid_count).astype(F32)
    col_cond = columns[:, 16:].reshape(8, TC, grid_count).astype(F32)
    basis_ranks = lax.dynamic_slice_in_dim(screen_basis, i * rank_quarter, rank_quarter, 1)

    def project(pairs, basis):
        flat = pairs.astype(BF16).reshape(-1, grid_count)
        return lax.dot_general(
            basis, flat, (((0,), (1,)), ((), ())), preferred_element_type=F32
        ).astype(BF16)

    val_part = project(col_val[:, None, :, None] * row_val[None, :, None, :], basis_ranks)
    cond_part = project(row_cond[None, :, :, None] * col_cond[:, None, None, :], basis_ranks)
    row_part = project(
        jnp.swapaxes(row_cond, 0, 1)[:, :, None] * row_val[None], screen_basis
    )
    row_part = row_part.reshape(8, 4, rank_part, 128)
    row_part = jnp.swapaxes(row_part, 1, 2).reshape(8, rank_part, 512)
    sent = jnp.concatenate(
        [
            val_part.reshape(8, rank_part, 1024),
            cond_part.reshape(8, rank_part, 1024),
            row_part,
        ],
        axis=2,
    )
    arrived = lax.all_to_all(sent, "ga", split_axis=0, concat_axis=0, tiled=True)
    summed = arrived.astype(F32).sum(axis=0)

    screen_part = lax.dynamic_slice_in_dim(
        screen, i * rank_quarter + k * rank_part, rank_part, 0
    )
    coulomb_part = lax.dynamic_slice_in_dim(coulomb, k * (R // 8), R // 8, 0)
    val_sum = (summed[:, :1024] * screen_part[:, None]).astype(BF16)
    cond_sum = summed[:, 1024:2048].astype(BF16)
    row_sum = summed[:, 2048:].reshape(rank_part, 4, 128)
    row_sum = (row_sum * coulomb_part.reshape(4, rank_part).T[:, :, None]).astype(BF16)

    proj_pieces = gather_pieces(jnp.stack([val_sum, cond_sum]), "cp")
    near = row_sum.reshape(1, rank_part, 512)
    for bits in (1, 2):
        near = jnp.concatenate([near, shift(near, "ga", lambda n, bits=bits: n ^ bits)])
    far = shift(near, "ga", lambda n: n ^ 6)
    basis_rows = lax.dynamic_slice_in_dim(screen_basis, i * quarter, quarter, 0)
    exchange = exchange_tiles(meta, ids, basis_rows, near, far, wave_pieces)

    order = jnp.arange(512, dtype=jnp.int32)
    source = (order // 8 % 8) * 64 + (order // 64) * 8 + order % 8
    order = (order[:, None] == source[None, :]).astype(BF16)
    tiles = kernel_tiles(meta, ids, order, exchange, proj_pieces)
    got = lax.all_to_all(tiles, ("vp", "ga"), split_axis=0, concat_axis=0, tiled=True)
    kernel = got.astype(F32).sum(axis=0).reshape(2, own_slots, 512)
    live_tile = (tile_owner[None, :] >= window_rows[:, None])[:, :, None]
    return jnp.where(live_tile, kernel, jnp.zeros_like(kernel))


def solution(mesh):
    in_specs = (
        P(("vp", "cp"), "ga"),
        P(("vp", "cp"), "ga"),
        P("ga", None),
        P(),
        P(),
        P(),
        P(("vp", "cp")),
    )
    out_specs = P(None, ("vp", "cp"), "ga")
    return jax.shard_map(shards, mesh=mesh, in_specs=in_specs, out_specs=out_specs, check_vma=False)
```

```python
import functools
import jax
import jax.numpy as jnp
from jax import lax
from jax.experimental import pallas as pl
from jax.experimental.pallas import tpu as pltpu
from jax.sharding import PartitionSpec as P

R = 1024
TV = 8
TC = 8
NCT = 64
F32 = jnp.float32
BF16 = jnp.bfloat16


def shift(array, axis, send_to):
    size = lax.axis_size(axis)
    return lax.ppermute(array, axis, [(n, send_to(n)) for n in range(size)])


def bands_of(tile):
    device = tile // 2
    return device // 8, device % 8, tile % 2


def pick_kernel(meta_ref, window_ref, columns_ref, mine_ref, other_ref, quarter_ref):
    i, j = meta_ref[0], meta_ref[1]
    width = 2 * mine_ref.shape[1]
    first_lane = pl.multiple_of(i * width, 128)
    picked = []
    for first in (0, 16):
        for q in range(2):
            block = window_ref[q]
            at, column, half = bands_of(block // NCT if first == 0 else block % NCT)
            both = columns_ref[at, first : first + 16, pl.ds(first_lane, width)].astype(F32)
            rows = jnp.where(half == 0, both[:8], both[8:])
            picked.append(jnp.where(column == j, rows, jnp.zeros_like(rows)))
    quarter_ref[...] = columns_ref[:, :, pl.ds(first_lane, width)]
    rows = jnp.concatenate(picked, axis=0)
    low, high = rows[:, : width // 2], rows[:, width // 2 :]
    mine_ref[...] = jnp.where(j % 2 == 0, low, high).astype(BF16)
    other_ref[...] = jnp.where(j % 2 == 0, high, low).astype(BF16)


def place_kernel(meta_ref, near_ref, next_ref, far_ref, out_ref):
    i, j = meta_ref[0], meta_ref[1]
    width = out_ref.shape[1] // 8
    for n, flip in enumerate((0, 1, 3, 2)):
        for half in range(2):
            start = (i ^ flip) * 2 + (j + half) % 2
            ref = (near_ref, next_ref, far_ref, far_ref)[n]
            at = half * width + (near_ref.shape[1] if n == 3 else 0)
            first = pl.multiple_of(start * width, 128)
            out_ref[:, pl.ds(first, width)] = ref[:, at : at + width]


def row_tiles(meta, window_rows, columns, tile_owner):
    width = columns.shape[2] // 8
    smem, vmem = (pl.BlockSpec(memory_space=m) for m in (pltpu.SMEM, pltpu.VMEM))
    part = jax.ShapeDtypeStruct((32, width), BF16)
    mine, other, quarter = pl.pallas_call(
        pick_kernel,
        out_shape=(part, part, jax.ShapeDtypeStruct((4, 32, 2 * width), BF16)),
        in_specs=[smem, smem, vmem],
        out_specs=(vmem, vmem, vmem),
        compiler_params=pltpu.CompilerParams(vmem_limit_bytes=16 * 2**20),
    )(meta, window_rows, columns)
    mine = mine + shift(other, "cp", lambda n: n ^ 1)
    mine = mine + shift(mine, "cp", lambda n: n ^ 2)
    mine = mine + shift(mine, "cp", lambda n: n ^ 6)
    quarter, mine = lax.optimization_barrier((quarter, mine))
    slots = tile_owner.shape[0]
    tiles = jnp.repeat(jnp.stack([tile_owner // NCT, tile_owner % NCT], axis=1), 64, axis=1)
    tiles = jnp.pad(tiles, ((0, 32 - slots), (0, 0))).astype(BF16)
    near = jnp.concatenate([mine, shift(mine, "cp", lambda n: n ^ 1), tiles], axis=1)
    beside = shift(near, "vp", lambda n: n ^ 1)
    far = shift(jnp.concatenate([near, beside], axis=1), "vp", lambda n: n ^ 3)
    rows = pl.pallas_call(
        place_kernel,
        out_shape=jax.ShapeDtypeStruct((32, columns.shape[2]), BF16),
        in_specs=[smem] + [vmem] * 3,
        out_specs=vmem,
        compiler_params=pltpu.CompilerParams(vmem_limit_bytes=16 * 2**20),
    )(meta, near, beside, far)
    tiles = [near[:slots, -128:], beside[:slots, -128:]]
    tiles += [far[:slots, near.shape[1] - 128 : near.shape[1]], far[:slots, -128:]]
    tiles = jnp.stack(tiles).astype(jnp.int32)
    return rows, quarter, tiles[:, :, 0] * NCT + tiles[:, :, 64]


def pair_block(left, right):
    product = left.astype(F32)[:, None, :] * right.astype(F32)[None, :, :]
    return product.reshape(-1, left.shape[1])


def owner_of(ids_ref, i, slot):
    own = ids_ref.shape[1]
    flip = i ^ (slot // own)
    return ids_ref[flip ^ (flip // 2), slot % own]


def sum_kernel(arrived_ref, scale_ref, proj_ref, row_ref):
    total = arrived_ref[0].astype(F32)
    for n in range(1, arrived_ref.shape[0]):
        total = total + arrived_ref[n].astype(F32)
    total = (total * scale_ref[...]).astype(BF16)
    width = proj_ref.shape[2]
    proj_ref[0] = total[:, :width]
    proj_ref[1] = total[:, width : 2 * width]
    for n in range(row_ref.shape[0]):
        row_ref[n] = total[:, 2 * width :]


def rank_sums(arrived, scale):
    groups, ranks, width = arrived.shape
    vmem = pl.BlockSpec(memory_space=pltpu.VMEM)
    return pl.pallas_call(
        sum_kernel,
        out_shape=(
            jax.ShapeDtypeStruct((2, ranks, 1024), BF16),
            jax.ShapeDtypeStruct((groups, ranks, width - 2048), BF16),
        ),
        in_specs=[vmem, vmem],
        out_specs=(vmem, vmem),
        compiler_params=pltpu.CompilerParams(vmem_limit_bytes=16 * 2**20),
    )(arrived, scale)


def exchange_kernel(meta_ref, ids_ref, whole_ref, row_ref, *refs):
    pieces, (out_ref, waves_ref, basis_ref, done_ref) = refs[:8], refs[8:]
    i, j = meta_ref[0], meta_ref[1]
    count = basis_ref.shape[0]
    first = pl.multiple_of(i * count, count)
    copy = pltpu.make_async_copy(whole_ref.at[pl.ds(first, count)], basis_ref, done_ref)
    copy.start()
    together = 4
    for flip in range(2):
        for n in range(4):
            source = ((j // 2 + 4 - n) % 4) * 2 + (j + flip) % 2
            waves_ref[pl.ds(source * 4, 4)] = pieces[4 * flip + n][...]
    copy.wait()
    potential = None
    for n in range(8):
        piece = row_ref[n]
        ranks = jnp.concatenate([piece[:, m * 128 : (m + 1) * 128] for m in range(4)], axis=0)
        basis = basis_ref[:, n * 128 : (n + 1) * 128]
        term = lax.dot_general(
            ranks, basis, (((0,), (1,)), ((), ())), preferred_element_type=F32
        )
        potential = term if potential is None else potential + term
    potential = potential.astype(BF16)

    def band_rows(first, tile):
        at, column, half = bands_of(tile)
        both = waves_ref[column * 4 + at, first : first + 16].astype(F32)
        return jnp.where(half == 0, both[:8], both[8:])

    for step in range(out_ref.shape[0] // together):
        pairs = []
        for n in range(together):
            owner = owner_of(ids_ref, i, step * together + n)
            left = band_rows(0, owner // NCT)
            right = band_rows(16, owner % NCT)
            pairs.append(pair_block(left, right).astype(BF16))
        pair = jnp.concatenate(pairs, axis=0)
        result = lax.dot_general(
            potential, pair, (((1,), (1,)), ((), ())), preferred_element_type=F32
        )
        for n in range(together):
            tile = result[:, n * 64 : (n + 1) * 64]
            out_ref[step * together + n] = jnp.concatenate(
                [tile[c * 16 : (c + 1) * 16] for c in range(8)], axis=1
            )


def exchange_tiles(meta, ids, basis, row_sums, pieces):
    slots = 4 * ids.shape[1]
    smem, vmem = (pl.BlockSpec(memory_space=m) for m in (pltpu.SMEM, pltpu.VMEM))
    return pl.pallas_call(
        exchange_kernel,
        out_shape=jax.ShapeDtypeStruct((slots, 16, 512), F32),
        in_specs=[smem, smem, pl.BlockSpec(memory_space=pl.ANY), vmem] + [vmem] * 8,
        out_specs=vmem,
        scratch_shapes=[
            pltpu.VMEM((32,) + pieces[0].shape[1:], BF16),
            pltpu.VMEM((basis.shape[0] // 4, basis.shape[1]), BF16),
            pltpu.SemaphoreType.DMA(()),
        ],
        compiler_params=pltpu.CompilerParams(vmem_limit_bytes=32 * 2**20),
        cost_estimate=pl.CostEstimate(
            flops=2 * slots * 64 * 128 * 768, bytes_accessed=2**22, transcendentals=0
        ),
    )(meta, ids, basis, row_sums, *pieces)


def direct_kernel(meta_ref, ids_ref, order_ref, exchange_ref, *refs):
    pieces, (out_ref, proj_ref, held_ref, total_ref) = refs[:8], refs[8:]
    i, j = meta_ref[0], meta_ref[1]
    own = ids_ref.shape[1]
    slots = 4 * own
    lane = lax.broadcasted_iota(jnp.int32, (8, 128), 1)
    for flip in range(2):
        for n in range(4):
            source = ((j // 2 + 4 - n) % 4) * 2 + (j + flip) % 2
            proj_ref[source] = pieces[4 * flip + n][...]

    def lanes_of(part, tile):
        at, column, half = bands_of(tile)
        first = pl.multiple_of((at * 2 + half) * 128, 128)
        return proj_ref[column, part, :, pl.ds(first, 128)]

    for slot in range(slots):
        owner = owner_of(ids_ref, i, slot)
        left = lanes_of(0, owner // NCT)
        right = lanes_of(1, owner % NCT)
        tile = lax.dot_general(
            left, right, (((0,), (0,)), ((), ())), preferred_element_type=F32
        )
        rows = []
        for q in range(2):
            blocks = []
            for m in range(4):
                even = tile[q * 64 + m * 16 : q * 64 + m * 16 + 8]
                odd = tile[q * 64 + m * 16 + 8 : q * 64 + m * 16 + 16]
                if q == 0:
                    odd = pltpu.roll(odd, 64, 1)
                else:
                    even = pltpu.roll(even, 64, 1)
                blocks.append(jnp.where(lane < 64, even, odd))
            rows.append(jnp.concatenate(blocks, axis=1))
        held_ref[slot] = jnp.concatenate(rows, axis=0).astype(BF16)
    for part in range(4):
        direct = jnp.dot(
            held_ref[part * own : (part + 1) * own].reshape(own * 16, 512),
            order_ref[...],
            preferred_element_type=F32,
        ).reshape(own, 16, 512)
        total = 2.0 * exchange_ref[part * own : (part + 1) * own] - direct
        for n in range(own):
            for q in range(2):
                for block in range(4):
                    total_ref[
                        part * 8 : (part + 1) * 8, block * 2 * own + q * own + n, :
                    ] = total[n, q * 8 : (q + 1) * 8, block * 128 : (block + 1) * 128]
    out_ref[...] = total_ref[...].astype(BF16)


def kernel_tiles(meta, ids, order, exchange, pieces):
    own = ids.shape[1]
    slots = 4 * own
    smem, vmem = (pl.BlockSpec(memory_space=m) for m in (pltpu.SMEM, pltpu.VMEM))
    return pl.pallas_call(
        direct_kernel,
        out_shape=jax.ShapeDtypeStruct((32, 8 * own, 128), BF16),
        in_specs=[smem, smem, vmem, vmem] + [vmem] * 8,
        out_specs=vmem,
        scratch_shapes=[
            pltpu.VMEM((8,) + pieces[0].shape, BF16),
            pltpu.VMEM((slots, 16, 512), BF16),
            pltpu.VMEM((32, 8 * own, 128), F32),
        ],
        compiler_params=pltpu.CompilerParams(vmem_limit_bytes=32 * 2**20),
    )(meta, ids, order, exchange, *pieces)


def shards(valence_wavefunction, cond_wave, screen_basis, screen, coulomb, window_rows, tile_owner):
    i = lax.axis_index("vp")
    j = lax.axis_index("cp")
    k = lax.axis_index("ga")
    meta = jnp.stack([i, j, k]).astype(jnp.int32)
    own_slots = tile_owner.shape[0]
    grid_count = valence_wavefunction.shape[1]
    quarter = grid_count // 4
    rank_quarter = R // 4
    rank_part = rank_quarter // 8

    waves = jnp.concatenate([valence_wavefunction, cond_wave], axis=0)
    columns = lax.all_gather(waves, "vp", axis=0)
    rows, quarter_waves, ids = row_tiles(meta, window_rows, columns, tile_owner)
    wave_pieces = [quarter_waves] + [
        shift(quarter_waves, "cp", lambda n, s=s: (n + 2 * s) % 8) for s in (2, 1, 3)
    ]

    row_val = rows[:16].reshape(2, TV, grid_count).astype(F32)
    row_cond = rows[16:].reshape(2, TC, grid_count).astype(F32)
    col_val = columns[:, :16].reshape(8, TV, grid_count).astype(F32)
    col_cond = columns[:, 16:].reshape(8, TC, grid_count).astype(F32)
    basis_ranks = lax.dynamic_slice_in_dim(screen_basis, i * rank_quarter, rank_quarter, 1)

    def project(pairs, basis):
        flat = pairs.astype(BF16).reshape(-1, grid_count)
        return lax.dot_general(
            basis, flat, (((0,), (1,)), ((), ())), preferred_element_type=F32
        ).astype(BF16)

    val_part = project(col_val[:, None, :, None] * row_val[None, :, None, :], basis_ranks)
    cond_part = project(row_cond[None, :, :, None] * col_cond[:, None, None, :], basis_ranks)
    row_part = project(
        jnp.swapaxes(row_cond, 0, 1)[:, :, None] * row_val[None], screen_basis
    )
    row_part = row_part.reshape(8, 4, rank_part, 128)
    row_part = jnp.swapaxes(row_part, 1, 2).reshape(8, rank_part, 512)
    sent = jnp.concatenate(
        [
            val_part.reshape(8, rank_part, 1024),
            cond_part.reshape(8, rank_part, 1024),
            row_part,
        ],
        axis=2,
    )
    sent, wave_pieces = lax.optimization_barrier((sent, wave_pieces))
    wave_pieces = [wave_pieces[n] for n in (0, 2, 1, 3)]
    wave_pieces = wave_pieces + [shift(a, "cp", lambda n: n ^ 1) for a in wave_pieces]
    screen_part = lax.dynamic_slice_in_dim(
        screen, i * rank_quarter + k * rank_part, rank_part, 0
    )
    coulomb_part = lax.dynamic_slice_in_dim(coulomb, k * (R // 8), R // 8, 0)
    scale = jnp.concatenate(
        [
            jnp.broadcast_to(screen_part[:, None], (rank_part, 1024)),
            jnp.ones((rank_part, 1024), F32),
            jnp.repeat(coulomb_part.reshape(4, rank_part).T, 128, axis=1),
        ],
        axis=1,
    )
    arrived = lax.all_to_all(sent, "ga", split_axis=0, concat_axis=0, tiled=True)
    arrived, ids, scale = lax.optimization_barrier((arrived, ids, scale))
    proj, row_copies = rank_sums(arrived, scale)
    step = [proj] + [
        shift(proj, "cp", lambda n, s=s: (n + 2 * s) % 8) for s in (1, 2, 3)
    ]
    row_sums = lax.all_to_all(row_copies, "ga", split_axis=0, concat_axis=0, tiled=True)
    exchange = exchange_tiles(meta, ids, screen_basis, row_sums, wave_pieces)

    step, exchange = lax.optimization_barrier((step, exchange))
    proj_pieces = step + [shift(a, "cp", lambda n: n ^ 1) for a in step]
    order = jnp.arange(512, dtype=jnp.int32)
    source = (order // 8 % 8) * 64 + (order // 64) * 8 + order % 8
    order = (order[:, None] == source[None, :]).astype(BF16)
    tiles = kernel_tiles(meta, ids, order, exchange, proj_pieces)
    got = lax.all_to_all(tiles, ("vp", "ga"), split_axis=0, concat_axis=0, tiled=True)
    kernel = got.astype(F32).sum(axis=0).reshape(4, 2, own_slots, 128)
    kernel = jnp.transpose(kernel, (1, 2, 0, 3)).reshape(2, own_slots, 512)
    live_tile = (tile_owner[None, :] >= window_rows[:, None])[:, :, None]
    return jnp.where(live_tile, kernel, jnp.zeros_like(kernel))


def solution(mesh):
    in_specs = (
        P(("vp", "cp"), "ga"),
        P(("vp", "cp"), "ga"),
        P("ga", None),
        P(),
        P(),
        P(),
        P(("vp", "cp")),
    )
    out_specs = P(None, ("vp", "cp"), "ga")
    return jax.shard_map(shards, mesh=mesh, in_specs=in_specs, out_specs=out_specs, check_vma=False)
```

```python
import functools
import jax
import jax.numpy as jnp
from jax import lax
from jax.experimental import pallas as pl
from jax.experimental.pallas import tpu as pltpu
from jax.sharding import PartitionSpec as P

R = 1024
TV = 8
TC = 8
NCT = 64
F32 = jnp.float32
BF16 = jnp.bfloat16


def shift(array, axis, send_to):
    size = lax.axis_size(axis)
    return lax.ppermute(array, axis, [(n, send_to(n)) for n in range(size)])


def bands_of(tile):
    device = tile // 2
    return device // 8, device % 8, tile % 2


def pick_kernel(meta_ref, columns_ref, mine_ref, other_ref, quarter_ref):
    i, j = meta_ref[0], meta_ref[1]
    width = 2 * mine_ref.shape[1]
    first_lane = pl.multiple_of(i * width, 128)
    picked = []
    for first in (0, 16):
        for q in range(2):
            block = meta_ref[3 + q]
            at, column, half = bands_of(block // NCT if first == 0 else block % NCT)
            both = columns_ref[at, first : first + 16, pl.ds(first_lane, width)].astype(F32)
            rows = jnp.where(half == 0, both[:8], both[8:])
            picked.append(jnp.where(column == j, rows, jnp.zeros_like(rows)))
    quarter_ref[...] = columns_ref[:, :, pl.ds(first_lane, width)]
    rows = jnp.concatenate(picked, axis=0)
    low, high = rows[:, : width // 2], rows[:, width // 2 :]
    mine_ref[...] = jnp.where(j % 2 == 0, low, high).astype(BF16)
    other_ref[...] = jnp.where(j % 2 == 0, high, low).astype(BF16)


def row_tiles(meta, columns, tile_owner):
    width = columns.shape[2] // 8
    smem, vmem = (pl.BlockSpec(memory_space=m) for m in (pltpu.SMEM, pltpu.VMEM))
    part = jax.ShapeDtypeStruct((32, width), BF16)
    mine, other, quarter = pl.pallas_call(
        pick_kernel,
        out_shape=(part, part, jax.ShapeDtypeStruct((4, 32, 2 * width), BF16)),
        in_specs=[smem, vmem],
        out_specs=(vmem, vmem, vmem),
        compiler_params=pltpu.CompilerParams(vmem_limit_bytes=16 * 2**20),
    )(meta, columns)
    mine = mine + shift(other, "cp", lambda n: n ^ 1)
    mine = mine + shift(mine, "cp", lambda n: n ^ 2)
    mine = mine + shift(mine, "cp", lambda n: n ^ 6)
    quarter, mine = lax.optimization_barrier((quarter, mine))
    slots = tile_owner.shape[0]
    tiles = jnp.repeat(jnp.stack([tile_owner // NCT, tile_owner % NCT], axis=1), 64, axis=1)
    tiles = jnp.pad(tiles, ((0, 32 - slots), (0, 0))).astype(BF16)
    near = jnp.concatenate([mine, shift(mine, "cp", lambda n: n ^ 1), tiles], axis=1)
    beside = shift(near, "vp", lambda n: n ^ 1)
    far = shift(jnp.concatenate([near, beside], axis=1), "vp", lambda n: n ^ 3)
    tiles = [near[:slots, -128:], beside[:slots, -128:]]
    tiles += [far[:slots, near.shape[1] - 128 : near.shape[1]], far[:slots, -128:]]
    tiles = jnp.stack(tiles).astype(jnp.int32)
    return (near, beside, far), quarter, tiles[:, :, 0] * NCT + tiles[:, :, 64]


def project_kernel(
    meta_ref, near_ref, next_ref, far_ref, columns_ref, whole_ref, out_ref,
    rows_ref, band_ref, pair_ref, basis_ref, done_ref,
):
    i, j = meta_ref[0], meta_ref[1]
    ranks = basis_ref.shape[2]
    copies = []
    for n in range(4):
        first = pl.multiple_of((i + n) % 4 * ranks, ranks)
        copies.append(
            pltpu.make_async_copy(
                whole_ref.at[:, pl.ds(first, ranks)], basis_ref.at[n], done_ref.at[n]
            )
        )
        copies[n].start()
    width = rows_ref.shape[1] // 8
    for n, flip in enumerate((0, 1, 3, 2)):
        for half in range(2):
            start = (i ^ flip) * 2 + (j + half) % 2
            ref = (near_ref, next_ref, far_ref, far_ref)[n]
            at = half * width + (near_ref.shape[1] if n == 3 else 0)
            first = pl.multiple_of(start * width, 128)
            rows_ref[:, pl.ds(first, width)] = ref[:, at : at + width].astype(F32)
    for kind in range(2):
        rows = rows_ref[kind * 16 : kind * 16 + 16]
        for at in range(4):
            slot = (kind * 4 + at) % 2
            band_ref[slot] = columns_ref[at, kind * 16 : kind * 16 + 16].astype(F32)
            for band in range(0, 16, 2):
                for q in range(2):
                    row = rows[q * 8 : q * 8 + 8]
                    first = band // 8 * 128 + q * 64 + band % 8 * 8
                    pair_ref[slot, first : first + 16] = jnp.concatenate(
                        [band_ref[slot, n : n + 1] * row for n in (band, band + 1)], axis=0
                    ).astype(BF16)
            if kind == 0 and at == 0:
                copies[0].wait()
            part = jnp.dot(pair_ref[slot], basis_ref[0], preferred_element_type=F32)
            part = part.T.astype(BF16).reshape(8, ranks // 8, 256)
            first = (kind * 4 + at) * 256
            out_ref[:, :, first : first + 256] = part
    rows = rows_ref[:16]
    upper = lax.broadcasted_iota(jnp.int32, rows.shape, 0) < 8
    for c in range(8):
        other = jnp.where(upper, rows_ref[16 + c : 17 + c], rows_ref[24 + c : 25 + c])
        pair_ref[0, c * 16 : c * 16 + 16] = (rows * other).astype(BF16)
    for n in range(4):
        if n:
            copies[n].wait()
        part = jnp.dot(pair_ref[0, :128], basis_ref[n], preferred_element_type=F32)
        part = part.astype(BF16)
        for m in range(4):
            for side in range(2):
                out_ref[(i + n) % 4 * 2 + side, :, 2048 + m * 128 : 2176 + m * 128] = part[
                    m * 32 : m * 32 + 32, side * 128 : side * 128 + 128
                ]


def project_bands(meta, row_parts, columns, basis):
    smem, vmem = (pl.BlockSpec(memory_space=m) for m in (pltpu.SMEM, pltpu.VMEM))
    grid_count = columns.shape[2]
    return pl.pallas_call(
        project_kernel,
        out_shape=jax.ShapeDtypeStruct((8, R // 32, 2560), BF16),
        in_specs=[smem] + [vmem] * 4 + [pl.BlockSpec(memory_space=pl.ANY)],
        out_specs=vmem,
        scratch_shapes=[
            pltpu.VMEM((32, grid_count), F32),
            pltpu.VMEM((2, 16, grid_count), F32),
            pltpu.VMEM((2, 256, grid_count), BF16),
            pltpu.VMEM((4, grid_count, R // 4), BF16),
            pltpu.SemaphoreType.DMA((4,)),
        ],
        compiler_params=pltpu.CompilerParams(vmem_limit_bytes=54 * 2**20),
        cost_estimate=pl.CostEstimate(
            flops=2 * 2560 * grid_count * R // 4, bytes_accessed=2**23, transcendentals=0
        ),
    )(meta, *row_parts, columns, basis)


def pair_block(left, right):
    product = left.astype(F32)[:, None, :] * right.astype(F32)[None, :, :]
    return product.reshape(-1, left.shape[1])


def owner_of(ids_ref, i, slot):
    own = ids_ref.shape[1]
    flip = i ^ (slot // own)
    return ids_ref[flip ^ (flip // 2), slot % own]


def sum_kernel(arrived_ref, scale_ref, proj_ref, row_ref):
    total = arrived_ref[0].astype(F32)
    for n in range(1, arrived_ref.shape[0]):
        total = total + arrived_ref[n].astype(F32)
    total = (total * scale_ref[...]).astype(BF16)
    width = proj_ref.shape[2]
    proj_ref[0] = total[:, :width]
    proj_ref[1] = total[:, width : 2 * width]
    for n in range(row_ref.shape[0]):
        row_ref[n] = total[:, 2 * width :]


def rank_sums(arrived, scale):
    groups, ranks, width = arrived.shape
    vmem = pl.BlockSpec(memory_space=pltpu.VMEM)
    return pl.pallas_call(
        sum_kernel,
        out_shape=(
            jax.ShapeDtypeStruct((2, ranks, 1024), BF16),
            jax.ShapeDtypeStruct((groups, ranks, width - 2048), BF16),
        ),
        in_specs=[vmem, vmem],
        out_specs=(vmem, vmem),
        compiler_params=pltpu.CompilerParams(vmem_limit_bytes=16 * 2**20),
    )(arrived, scale)


def exchange_kernel(meta_ref, ids_ref, whole_ref, row_ref, *refs):
    pieces, (out_ref, waves_ref, basis_ref, done_ref) = refs[:8], refs[8:]
    i, j = meta_ref[0], meta_ref[1]
    count = basis_ref.shape[0]
    first = pl.multiple_of(i * count, count)
    copy = pltpu.make_async_copy(whole_ref.at[pl.ds(first, count)], basis_ref, done_ref)
    copy.start()
    together = 4
    for flip in range(2):
        for n in range(4):
            source = ((j // 2 + 4 - n) % 4) * 2 + (j + flip) % 2
            waves_ref[pl.ds(source * 4, 4)] = pieces[4 * flip + n][...]
    copy.wait()
    potential = None
    for n in range(8):
        piece = row_ref[n]
        ranks = jnp.concatenate([piece[:, m * 128 : (m + 1) * 128] for m in range(4)], axis=0)
        basis = basis_ref[:, n * 128 : (n + 1) * 128]
        term = lax.dot_general(
            ranks, basis, (((1,), (1,)), ((), ())), preferred_element_type=F32
        )
        potential = term if potential is None else potential + term
    potential = potential.astype(BF16)

    def band_rows(first, tile):
        at, column, half = bands_of(tile)
        both = waves_ref[column * 4 + at, first : first + 16].astype(F32)
        return jnp.where(half == 0, both[:8], both[8:])

    for step in range(out_ref.shape[0] // together):
        pairs = []
        for n in range(together):
            owner = owner_of(ids_ref, i, step * together + n)
            left = band_rows(0, owner // NCT)
            right = band_rows(16, owner % NCT)
            pairs.append(pair_block(left, right).astype(BF16))
        pair = jnp.concatenate(pairs, axis=0)
        result = lax.dot_general(
            potential, pair, (((1,), (1,)), ((), ())), preferred_element_type=F32
        )
        for n in range(together):
            tile = result[:, n * 64 : (n + 1) * 64]
            out_ref[step * together + n] = jnp.concatenate(
                [tile[c * 16 : (c + 1) * 16] for c in range(8)], axis=1
            )


def exchange_tiles(meta, ids, basis, row_sums, pieces):
    slots = 4 * ids.shape[1]
    smem, vmem = (pl.BlockSpec(memory_space=m) for m in (pltpu.SMEM, pltpu.VMEM))
    return pl.pallas_call(
        exchange_kernel,
        out_shape=jax.ShapeDtypeStruct((slots, 16, 512), F32),
        in_specs=[smem, smem, pl.BlockSpec(memory_space=pl.ANY), vmem] + [vmem] * 8,
        out_specs=vmem,
        scratch_shapes=[
            pltpu.VMEM((32,) + pieces[0].shape[1:], BF16),
            pltpu.VMEM((basis.shape[0] // 4, basis.shape[1]), BF16),
            pltpu.SemaphoreType.DMA(()),
        ],
        compiler_params=pltpu.CompilerParams(vmem_limit_bytes=32 * 2**20),
        cost_estimate=pl.CostEstimate(
            flops=2 * slots * 64 * 128 * 768, bytes_accessed=2**22, transcendentals=0
        ),
    )(meta, ids, basis, row_sums, *pieces)


def direct_kernel(meta_ref, ids_ref, order_ref, exchange_ref, *refs):
    pieces, (out_ref, proj_ref, held_ref, total_ref) = refs[:8], refs[8:]
    i, j = meta_ref[0], meta_ref[1]
    own = ids_ref.shape[1]
    slots = 4 * own
    lane = lax.broadcasted_iota(jnp.int32, (8, 128), 1)
    for flip in range(2):
        for n in range(4):
            source = ((j // 2 + 4 - n) % 4) * 2 + (j + flip) % 2
            proj_ref[source] = pieces[4 * flip + n][...]

    def lanes_of(part, tile):
        at, column, half = bands_of(tile)
        first = pl.multiple_of((at * 2 + half) * 128, 128)
        return proj_ref[column, part, :, pl.ds(first, 128)]

    for slot in range(slots):
        owner = owner_of(ids_ref, i, slot)
        left = lanes_of(0, owner // NCT)
        right = lanes_of(1, owner % NCT)
        tile = lax.dot_general(
            left, right, (((0,), (0,)), ((), ())), preferred_element_type=F32
        )
        rows = []
        for q in range(2):
            blocks = []
            for m in range(4):
                even = tile[q * 64 + m * 16 : q * 64 + m * 16 + 8]
                odd = tile[q * 64 + m * 16 + 8 : q * 64 + m * 16 + 16]
                if q == 0:
                    odd = pltpu.roll(odd, 64, 1)
                else:
                    even = pltpu.roll(even, 64, 1)
                blocks.append(jnp.where(lane < 64, even, odd))
            rows.append(jnp.concatenate(blocks, axis=1))
        held_ref[slot] = jnp.concatenate(rows, axis=0).astype(BF16)
    for part in range(4):
        direct = jnp.dot(
            held_ref[part * own : (part + 1) * own].reshape(own * 16, 512),
            order_ref[...],
            preferred_element_type=F32,
        ).reshape(own, 16, 512)
        total = 2.0 * exchange_ref[part * own : (part + 1) * own] - direct
        for n in range(own):
            for q in range(2):
                for block in range(4):
                    total_ref[
                        part * 8 : (part + 1) * 8, block * 2 * own + q * own + n, :
                    ] = total[n, q * 8 : (q + 1) * 8, block * 128 : (block + 1) * 128]
    out_ref[...] = total_ref[...].astype(BF16)


def kernel_tiles(meta, ids, order, exchange, pieces):
    own = ids.shape[1]
    slots = 4 * own
    smem, vmem = (pl.BlockSpec(memory_space=m) for m in (pltpu.SMEM, pltpu.VMEM))
    return pl.pallas_call(
        direct_kernel,
        out_shape=jax.ShapeDtypeStruct((32, 8 * own, 128), BF16),
        in_specs=[smem, smem, vmem, vmem] + [vmem] * 8,
        out_specs=vmem,
        scratch_shapes=[
            pltpu.VMEM((8,) + pieces[0].shape, BF16),
            pltpu.VMEM((slots, 16, 512), BF16),
            pltpu.VMEM((32, 8 * own, 128), F32),
        ],
        compiler_params=pltpu.CompilerParams(vmem_limit_bytes=32 * 2**20),
    )(meta, ids, order, exchange, *pieces)


def shards(valence_wavefunction, cond_wave, screen_basis, screen, coulomb, window_rows, tile_owner):
    i = lax.axis_index("vp")
    j = lax.axis_index("cp")
    k = lax.axis_index("ga")
    meta = jnp.concatenate([jnp.stack([i, j, k]).astype(jnp.int32), window_rows])
    own_slots = tile_owner.shape[0]
    grid_count = valence_wavefunction.shape[1]
    quarter = grid_count // 4
    rank_quarter = R // 4
    rank_part = rank_quarter // 8

    waves = jnp.concatenate([valence_wavefunction, cond_wave], axis=0)
    columns = lax.all_gather(waves, "vp", axis=0)
    row_parts, quarter_waves, ids = row_tiles(meta, columns, tile_owner)
    wave_pieces = [quarter_waves] + [
        shift(quarter_waves, "cp", lambda n, s=s: (n + 2 * s) % 8) for s in (2, 1, 3)
    ]

    row_parts, wave_pieces[1] = lax.optimization_barrier((row_parts, wave_pieces[1]))
    sent = project_bands(meta, row_parts, columns, screen_basis)
    sent, wave_pieces[1], wave_pieces[2], wave_pieces[3] = lax.optimization_barrier(
        (sent, wave_pieces[1], wave_pieces[2], wave_pieces[3])
    )
    wave_pieces = [wave_pieces[n] for n in (0, 2, 1, 3)]
    wave_pieces = wave_pieces + [shift(a, "cp", lambda n: n ^ 1) for a in wave_pieces]
    screen_part = lax.dynamic_slice_in_dim(
        screen, i * rank_quarter + k * rank_part, rank_part, 0
    )
    coulomb_part = lax.dynamic_slice_in_dim(coulomb, k * (R // 8), R // 8, 0)
    scale = jnp.concatenate(
        [
            jnp.broadcast_to(screen_part[:, None], (rank_part, 1024)),
            jnp.ones((rank_part, 1024), F32),
            jnp.tile(jnp.broadcast_to(coulomb_part, (rank_part, R // 8)), (1, 4)),
        ],
        axis=1,
    )
    arrived = lax.all_to_all(sent, "ga", split_axis=0, concat_axis=0, tiled=True)
    arrived, ids, scale = lax.optimization_barrier((arrived, ids, scale))
    proj, row_copies = rank_sums(arrived, scale)
    step = [proj] + [
        shift(proj, "cp", lambda n, s=s: (n + 2 * s) % 8) for s in (1, 2, 3)
    ]
    row_sums = lax.all_to_all(row_copies, "ga", split_axis=0, concat_axis=0, tiled=True)
    exchange = exchange_tiles(meta, ids, screen_basis, row_sums, wave_pieces)

    step, exchange = lax.optimization_barrier((step, exchange))
    proj_pieces = step + [shift(a, "cp", lambda n: n ^ 1) for a in step]
    order = jnp.arange(512, dtype=jnp.int32)
    source = (order // 8 % 8) * 64 + (order % 8) * 8 + order // 64
    order = (order[:, None] == source[None, :]).astype(BF16)
    tiles = kernel_tiles(meta, ids, order, exchange, proj_pieces)
    got = lax.all_to_all(tiles, ("vp", "ga"), split_axis=0, concat_axis=0, tiled=True)
    kernel = got.astype(F32).sum(axis=0).reshape(4, 2, own_slots, 128)
    kernel = jnp.transpose(kernel, (1, 2, 0, 3)).reshape(2, own_slots, 512)
    live_tile = (tile_owner[None, :] >= window_rows[:, None])[:, :, None]
    return jnp.where(live_tile, kernel, jnp.zeros_like(kernel))


def solution(mesh):
    in_specs = (
        P(("vp", "cp"), "ga"),
        P(("vp", "cp"), "ga"),
        P("ga", None),
        P(),
        P(),
        P(),
        P(("vp", "cp")),
    )
    out_specs = P(None, ("vp", "cp"), "ga")
    return jax.shard_map(shards, mesh=mesh, in_specs=in_specs, out_specs=out_specs, check_vma=False)
```

```python
import functools
import jax
import jax.numpy as jnp
from jax import lax
from jax.experimental import pallas as pl
from jax.experimental.pallas import tpu as pltpu
from jax.sharding import PartitionSpec as P

R = 1024
TV = 8
TC = 8
NCT = 64
F32 = jnp.float32
BF16 = jnp.bfloat16


def shift(array, axis, send_to):
    size = lax.axis_size(axis)
    return lax.ppermute(array, axis, [(n, send_to(n)) for n in range(size)])


def bands_of(tile):
    device = tile // 2
    return device // 8, device % 8, tile % 2


def pick_kernel(meta_ref, columns_ref, mine_ref, quarter_ref):
    i, j = meta_ref[0], meta_ref[1]
    width = mine_ref.shape[1]
    first_lane = pl.multiple_of(i * width, 128)
    picked = []
    for first in (0, 16):
        for q in range(2):
            block = meta_ref[3 + q]
            at, column, half = bands_of(block // NCT if first == 0 else block % NCT)
            both = columns_ref[at, first : first + 16, pl.ds(first_lane, width)].astype(F32)
            rows = jnp.where(half == 0, both[:8], both[8:])
            picked.append(jnp.where(column == j, rows, jnp.zeros_like(rows)))
    quarter_ref[...] = columns_ref[:, :, pl.ds(first_lane, width)]
    mine_ref[...] = jnp.concatenate(picked, axis=0).astype(BF16)


def row_tiles(meta, columns, tile_owner):
    width = columns.shape[2] // 4
    smem, vmem = (pl.BlockSpec(memory_space=m) for m in (pltpu.SMEM, pltpu.VMEM))
    mine, quarter = pl.pallas_call(
        pick_kernel,
        out_shape=(
            jax.ShapeDtypeStruct((32, width), BF16),
            jax.ShapeDtypeStruct((4, 32, width), BF16),
        ),
        in_specs=[smem, vmem],
        out_specs=(vmem, vmem),
        compiler_params=pltpu.CompilerParams(vmem_limit_bytes=16 * 2**20),
    )(meta, columns)
    mine = mine + shift(mine, "cp", lambda n: n ^ 2)
    quarter, mine = lax.optimization_barrier((quarter, mine))
    mine = mine + shift(mine, "cp", lambda n: n ^ 6)
    mine = mine + shift(mine, "cp", lambda n: n ^ 1)
    slots = tile_owner.shape[0]
    tiles = jnp.repeat(jnp.stack([tile_owner // NCT, tile_owner % NCT], axis=1), 64, axis=1)
    tiles = jnp.pad(tiles, ((0, 32 - slots), (0, 0))).astype(BF16)
    near = jnp.concatenate([mine, tiles], axis=1)
    beside = shift(near, "vp", lambda n: n ^ 1)
    across = shift(quarter, "cp", lambda n: (n + 4) % 8)
    beside, across = lax.optimization_barrier((beside, across))
    far = shift(jnp.concatenate([near, beside], axis=1), "vp", lambda n: n ^ 3)
    tiles = [near[:slots, -128:], beside[:slots, -128:]]
    tiles += [far[:slots, near.shape[1] - 128 : near.shape[1]], far[:slots, -128:]]
    tiles = jnp.stack(tiles).astype(jnp.int32)
    return (near, beside, far), (quarter, across), tiles[:, :, 0] * NCT + tiles[:, :, 64]


def project_kernel(
    meta_ref, near_ref, next_ref, far_ref, columns_ref, whole_ref, out_ref,
    rows_ref, band_ref, pair_ref, basis_ref, done_ref,
):
    i = meta_ref[0]
    ranks = basis_ref.shape[2]
    copies = []
    for n in range(4):
        first = pl.multiple_of((i + n) % 4 * ranks, ranks)
        copies.append(
            pltpu.make_async_copy(
                whole_ref.at[:, pl.ds(first, ranks)], basis_ref.at[n], done_ref.at[n]
            )
        )
        copies[n].start()
    width = rows_ref.shape[1] // 4
    for n, flip in enumerate((0, 1, 3, 2)):
        ref = (near_ref, next_ref, far_ref, far_ref)[n]
        at = near_ref.shape[1] if n == 3 else 0
        first = pl.multiple_of((i ^ flip) * width, 128)
        rows_ref[:, pl.ds(first, width)] = ref[:, at : at + width].astype(F32)
    for kind in range(2):
        rows = rows_ref[kind * 16 : kind * 16 + 16]
        for at in range(4):
            slot = (kind * 4 + at) % 2
            band_ref[slot] = columns_ref[at, kind * 16 : kind * 16 + 16].astype(F32)
            for band in range(0, 16, 2):
                for q in range(2):
                    row = rows[q * 8 : q * 8 + 8]
                    first = band // 8 * 128 + q * 64 + band % 8 * 8
                    pair_ref[slot, first : first + 16] = jnp.concatenate(
                        [band_ref[slot, n : n + 1] * row for n in (band, band + 1)], axis=0
                    ).astype(BF16)
            if kind == 0 and at == 0:
                copies[0].wait()
            part = jnp.dot(pair_ref[slot], basis_ref[0], preferred_element_type=F32)
            part = part.T.astype(BF16).reshape(8, ranks // 8, 256)
            first = (kind * 4 + at) * 256
            out_ref[:, :, first : first + 256] = part
    rows = rows_ref[:16]
    upper = lax.broadcasted_iota(jnp.int32, rows.shape, 0) < 8
    for c in range(8):
        other = jnp.where(upper, rows_ref[16 + c : 17 + c], rows_ref[24 + c : 25 + c])
        pair_ref[0, c * 16 : c * 16 + 16] = (rows * other).astype(BF16)
    for n in range(4):
        if n:
            copies[n].wait()
        part = jnp.dot(pair_ref[0, :128], basis_ref[n], preferred_element_type=F32)
        part = part.astype(BF16)
        for m in range(4):
            for side in range(2):
                out_ref[(i + n) % 4 * 2 + side, :, 2048 + m * 128 : 2176 + m * 128] = part[
                    m * 32 : m * 32 + 32, side * 128 : side * 128 + 128
                ]


def project_bands(meta, row_parts, columns, basis):
    smem, vmem = (pl.BlockSpec(memory_space=m) for m in (pltpu.SMEM, pltpu.VMEM))
    grid_count = columns.shape[2]
    return pl.pallas_call(
        project_kernel,
        out_shape=jax.ShapeDtypeStruct((8, R // 32, 2560), BF16),
        in_specs=[smem] + [vmem] * 4 + [pl.BlockSpec(memory_space=pl.ANY)],
        out_specs=vmem,
        scratch_shapes=[
            pltpu.VMEM((32, grid_count), F32),
            pltpu.VMEM((2, 16, grid_count), F32),
            pltpu.VMEM((2, 256, grid_count), BF16),
            pltpu.VMEM((4, grid_count, R // 4), BF16),
            pltpu.SemaphoreType.DMA((4,)),
        ],
        compiler_params=pltpu.CompilerParams(vmem_limit_bytes=54 * 2**20),
        cost_estimate=pl.CostEstimate(
            flops=2 * 2560 * grid_count * R // 4, bytes_accessed=2**23, transcendentals=0
        ),
    )(meta, *row_parts, columns, basis)


def pair_block(left, right):
    product = left.astype(F32)[:, None, :] * right.astype(F32)[None, :, :]
    return product.reshape(-1, left.shape[1])


def owner_of(ids_ref, i, slot):
    own = ids_ref.shape[1]
    flip = i ^ (slot // own)
    return ids_ref[flip ^ (flip // 2), slot % own]


def sum_kernel(arrived_ref, scale_ref, proj_ref, row_ref):
    total = arrived_ref[0].astype(F32)
    for n in range(1, arrived_ref.shape[0]):
        total = total + arrived_ref[n].astype(F32)
    total = (total * scale_ref[...]).astype(BF16)
    width = proj_ref.shape[2]
    proj_ref[0] = total[:, :width]
    proj_ref[1] = total[:, width : 2 * width]
    for n in range(row_ref.shape[0]):
        row_ref[n] = total[:, 2 * width :]


def rank_sums(arrived, scale):
    groups, ranks, width = arrived.shape
    vmem = pl.BlockSpec(memory_space=pltpu.VMEM)
    return pl.pallas_call(
        sum_kernel,
        out_shape=(
            jax.ShapeDtypeStruct((2, ranks, 1024), BF16),
            jax.ShapeDtypeStruct((groups, ranks, width - 2048), BF16),
        ),
        in_specs=[vmem, vmem],
        out_specs=(vmem, vmem),
        compiler_params=pltpu.CompilerParams(vmem_limit_bytes=16 * 2**20),
    )(arrived, scale)


def exchange_kernel(meta_ref, ids_ref, whole_ref, row_ref, *refs):
    pieces, (out_ref, waves_ref, basis_ref, done_ref) = refs[:8], refs[8:]
    i, j = meta_ref[0], meta_ref[1]
    count = basis_ref.shape[0]
    first = pl.multiple_of(i * count, count)
    copy = pltpu.make_async_copy(whole_ref.at[pl.ds(first, count)], basis_ref, done_ref)
    copy.start()
    together = 4
    for flip in range(2):
        for n in range(4):
            source = ((j // 2 + 4 - n) % 4) * 2 + (j + flip) % 2
            waves_ref[pl.ds(source * 4, 4)] = pieces[4 * flip + n][...]
    copy.wait()
    potential = None
    for n in range(8):
        piece = row_ref[n]
        ranks = jnp.concatenate([piece[:, m * 128 : (m + 1) * 128] for m in range(4)], axis=0)
        basis = basis_ref[:, n * 128 : (n + 1) * 128]
        term = lax.dot_general(
            ranks, basis, (((1,), (1,)), ((), ())), preferred_element_type=F32
        )
        potential = term if potential is None else potential + term
    potential = potential.astype(BF16)

    def band_rows(first, tile):
        at, column, half = bands_of(tile)
        both = waves_ref[column * 4 + at, first : first + 16].astype(F32)
        return jnp.where(half == 0, both[:8], both[8:])

    for step in range(out_ref.shape[0] // together):
        pairs = []
        for n in range(together):
            owner = owner_of(ids_ref, i, step * together + n)
            left = band_rows(0, owner // NCT)
            right = band_rows(16, owner % NCT)
            pairs.append(pair_block(left, right).astype(BF16))
        pair = jnp.concatenate(pairs, axis=0)
        result = lax.dot_general(
            potential, pair, (((1,), (1,)), ((), ())), preferred_element_type=F32
        )
        for n in range(together):
            tile = result[:, n * 64 : (n + 1) * 64]
            out_ref[step * together + n] = jnp.concatenate(
                [tile[c * 16 : (c + 1) * 16] for c in range(8)], axis=1
            )


def exchange_tiles(meta, ids, basis, row_sums, pieces):
    slots = 4 * ids.shape[1]
    smem, vmem = (pl.BlockSpec(memory_space=m) for m in (pltpu.SMEM, pltpu.VMEM))
    return pl.pallas_call(
        exchange_kernel,
        out_shape=jax.ShapeDtypeStruct((slots, 16, 512), F32),
        in_specs=[smem, smem, pl.BlockSpec(memory_space=pl.ANY), vmem] + [vmem] * 8,
        out_specs=vmem,
        scratch_shapes=[
            pltpu.VMEM((32,) + pieces[0].shape[1:], BF16),
            pltpu.VMEM((basis.shape[0] // 4, basis.shape[1]), BF16),
            pltpu.SemaphoreType.DMA(()),
        ],
        compiler_params=pltpu.CompilerParams(vmem_limit_bytes=32 * 2**20),
        cost_estimate=pl.CostEstimate(
            flops=2 * slots * 64 * 128 * 768, bytes_accessed=2**22, transcendentals=0
        ),
    )(meta, ids, basis, row_sums, *pieces)


def direct_kernel(meta_ref, ids_ref, order_ref, exchange_ref, *refs):
    pieces, (out_ref, proj_ref, held_ref, total_ref) = refs[:8], refs[8:]
    i, j = meta_ref[0], meta_ref[1]
    own = ids_ref.shape[1]
    slots = 4 * own
    lane = lax.broadcasted_iota(jnp.int32, (8, 128), 1)
    for flip in range(2):
        for n in range(4):
            source = ((j // 2 + 4 - n) % 4) * 2 + (j + flip) % 2
            proj_ref[source] = pieces[4 * flip + n][...]

    def lanes_of(part, tile):
        at, column, half = bands_of(tile)
        first = pl.multiple_of((at * 2 + half) * 128, 128)
        return proj_ref[column, part, :, pl.ds(first, 128)]

    for slot in range(slots):
        owner = owner_of(ids_ref, i, slot)
        left = lanes_of(0, owner // NCT)
        right = lanes_of(1, owner % NCT)
        tile = lax.dot_general(
            left, right, (((0,), (0,)), ((), ())), preferred_element_type=F32
        )
        rows = []
        for q in range(2):
            blocks = []
            for m in range(4):
                even = tile[q * 64 + m * 16 : q * 64 + m * 16 + 8]
                odd = tile[q * 64 + m * 16 + 8 : q * 64 + m * 16 + 16]
                if q == 0:
                    odd = pltpu.roll(odd, 64, 1)
                else:
                    even = pltpu.roll(even, 64, 1)
                blocks.append(jnp.where(lane < 64, even, odd))
            rows.append(jnp.concatenate(blocks, axis=1))
        held_ref[slot] = jnp.concatenate(rows, axis=0).astype(BF16)
    for part in range(4):
        direct = jnp.dot(
            held_ref[part * own : (part + 1) * own].reshape(own * 16, 512),
            order_ref[...],
            preferred_element_type=F32,
        ).reshape(own, 16, 512)
        total = 2.0 * exchange_ref[part * own : (part + 1) * own] - direct
        for n in range(own):
            for q in range(2):
                for block in range(4):
                    total_ref[
                        part * 8 : (part + 1) * 8, block * 2 * own + q * own + n, :
                    ] = total[n, q * 8 : (q + 1) * 8, block * 128 : (block + 1) * 128]
    out_ref[...] = total_ref[...].astype(BF16)


def kernel_tiles(meta, ids, order, exchange, pieces):
    own = ids.shape[1]
    slots = 4 * own
    smem, vmem = (pl.BlockSpec(memory_space=m) for m in (pltpu.SMEM, pltpu.VMEM))
    return pl.pallas_call(
        direct_kernel,
        out_shape=jax.ShapeDtypeStruct((32, 8 * own, 128), BF16),
        in_specs=[smem, smem, vmem, vmem] + [vmem] * 8,
        out_specs=vmem,
        scratch_shapes=[
            pltpu.VMEM((8,) + pieces[0].shape, BF16),
            pltpu.VMEM((slots, 16, 512), BF16),
            pltpu.VMEM((32, 8 * own, 128), F32),
        ],
        compiler_params=pltpu.CompilerParams(vmem_limit_bytes=32 * 2**20),
    )(meta, ids, order, exchange, *pieces)


def shards(valence_wavefunction, cond_wave, screen_basis, screen, coulomb, window_rows, tile_owner):
    i = lax.axis_index("vp")
    j = lax.axis_index("cp")
    k = lax.axis_index("ga")
    meta = jnp.concatenate([jnp.stack([i, j, k]).astype(jnp.int32), window_rows])
    own_slots = tile_owner.shape[0]
    grid_count = valence_wavefunction.shape[1]
    quarter = grid_count // 4
    rank_quarter = R // 4
    rank_part = rank_quarter // 8

    waves = jnp.concatenate([valence_wavefunction, cond_wave], axis=0)
    columns = lax.all_gather(waves, "vp", axis=0)
    row_parts, quarter_waves, ids = row_tiles(meta, columns, tile_owner)
    wave_pieces = list(quarter_waves) + [
        shift(quarter_waves[0], "cp", lambda n, s=s: (n + 2 * s) % 8) for s in (1, 3)
    ]

    sent = project_bands(meta, row_parts, columns, screen_basis)
    sent, wave_pieces[1], wave_pieces[2], wave_pieces[3] = lax.optimization_barrier(
        (sent, wave_pieces[1], wave_pieces[2], wave_pieces[3])
    )
    wave_pieces = [wave_pieces[n] for n in (0, 2, 1, 3)]
    wave_pieces = wave_pieces + [shift(a, "cp", lambda n: n ^ 1) for a in wave_pieces]
    screen_part = lax.dynamic_slice_in_dim(
        screen, i * rank_quarter + k * rank_part, rank_part, 0
    )
    coulomb_part = lax.dynamic_slice_in_dim(coulomb, k * (R // 8), R // 8, 0)
    scale = jnp.concatenate(
        [
            jnp.broadcast_to(screen_part[:, None], (rank_part, 1024)),
            jnp.ones((rank_part, 1024), F32),
            jnp.tile(jnp.broadcast_to(coulomb_part, (rank_part, R // 8)), (1, 4)),
        ],
        axis=1,
    )
    arrived = lax.all_to_all(sent, "ga", split_axis=0, concat_axis=0, tiled=True)
    arrived, ids, scale = lax.optimization_barrier((arrived, ids, scale))
    proj, row_copies = rank_sums(arrived, scale)
    step = [proj] + [
        shift(proj, "cp", lambda n, s=s: (n + 2 * s) % 8) for s in (1, 2, 3)
    ]
    row_sums = lax.all_to_all(row_copies, "ga", split_axis=0, concat_axis=0, tiled=True)
    exchange = exchange_tiles(meta, ids, screen_basis, row_sums, wave_pieces)

    step, exchange = lax.optimization_barrier((step, exchange))
    proj_pieces = step + [shift(a, "cp", lambda n: n ^ 1) for a in step]
    order = jnp.arange(512, dtype=jnp.int32)
    source = (order // 8 % 8) * 64 + (order % 8) * 8 + order // 64
    order = (order[:, None] == source[None, :]).astype(BF16)
    tiles = kernel_tiles(meta, ids, order, exchange, proj_pieces)
    got = lax.all_to_all(tiles, ("vp", "ga"), split_axis=0, concat_axis=0, tiled=True)
    kernel = got.astype(F32).sum(axis=0).reshape(4, 2, own_slots, 128)
    kernel = jnp.transpose(kernel, (1, 2, 0, 3)).reshape(2, own_slots, 512)
    live_tile = (tile_owner[None, :] >= window_rows[:, None])[:, :, None]
    return jnp.where(live_tile, kernel, jnp.zeros_like(kernel))


def solution(mesh):
    in_specs = (
        P(("vp", "cp"), "ga"),
        P(("vp", "cp"), "ga"),
        P("ga", None),
        P(),
        P(),
        P(),
        P(("vp", "cp")),
    )
    out_specs = P(None, ("vp", "cp"), "ga")
    return jax.shard_map(shards, mesh=mesh, in_specs=in_specs, out_specs=out_specs, check_vma=False)
```
